256 devices in a mesh: dom: 64 (over z, y, core), blk: 4 (over x).
Axes of the slice: x: 4, y: 4, z: 8, core: 2. Of those that a mesh axis runs over, the one named last changes fastest.
Arguments:
- current: bfloat16 [1048576, 128], P(('dom', 'blk')), may hold values from -6 to 6
- resistivity: bfloat16 [1048576], P(('dom', 'blk')), may hold values from 0.5 to 4
- temp_coef: bfloat16 [1048576], P(('dom', 'blk')), may hold values from 0.099609375 to 0.5
- dest_part: int32 [1048576, 1], P(('dom', 'blk')), may hold values from 0 to 63; in each aligned block of 4096 rows (0 to 4095, 4096 to 8191, ...) at most 128 rows name the same one
- dest_row: int32 [1048576], P(('dom', 'blk')), may hold values from 0 to 2047
- temp_old: float32 [524288, 128], P(('dom', 'blk')), may hold values from -6 to 6
- heat_cap: float32 [524288], P(('dom', 'blk')), may hold values from 0.25 to 2
- conduction: bfloat16 [8192, 64, 1024], P(('dom', 'blk'))
- block_cols: int32 [8192, 16], P(('dom', 'blk')), may hold values from 0 to 8191, as said below
Outputs:
- temperature: float32 [524288, 128], P(('dom', 'blk'))
- resist_new: bfloat16 [1048576, 128], P(('dom', 'blk'))
The draws below stay inside these ranges and needn't reach their ends.
Inputs may be any that keep to these rules, and one draw needn't show every extreme that they name: `dest_part`: the rows of one device name each partition at most 128 times; in every draw some device's rows name some partition exactly 128 times. `block_cols`: column 0 of block row r is r itself; the other 15 entries are distinct blocks r + o mod 8192 with 0 < |o| <= 12.
All inputs are finite; a program needn't handle non-finite values.
Results may differ from the reference program's by a relative error of at most 0.001.
The reference program's roundings to bfloat16 on the way (of `field_low`) count: a program that leaves them out, or rounds other values in their place, can miss the bound.
Values may be sent and summed in bfloat16 or wider, within the bound.
No kernel may reach another device: no remote copies, remote signals or barrier semaphores. Data moves between devices by JAX's collectives and lax.ppermute only.
A program may use at most 128 MiB of HBM per device.

```python
import math
import jax
import jax.numpy as jnp
import numpy as np

W = 128
BS = 64
K = 16
HB = 12
SWEEPS = 2
E_DEV = 4096
E_TOTAL = 1048576
NB_TOTAL = 8192
NODES_DEV = 2048
NODES = 524288
CAP = 128
N_DOM = 64
N_BLK = 4


def draw_block_cols(key, part):
    scores = jax.random.randint(jax.random.fold_in(key, 11), (NB_TOTAL, 2 * HB), 0, 1 << 20)
    scores = scores * (2 * HB) + jnp.arange(2 * HB, dtype=jnp.int32)[None, :]
    chosen = jnp.argsort(scores, axis=1)[:, :K - 1].astype(jnp.int32)
    offsets = jnp.where(chosen < HB, chosen - HB, chosen - HB + 1)
    base_rows = jnp.arange(NB_TOTAL, dtype=jnp.int32)[:, None]
    return jnp.concatenate([base_rows, jnp.mod(base_rows + offsets, NB_TOTAL)], axis=1).astype(jnp.int32)


def draw_conduction(key, part):
    shape_full = (NB_TOTAL, BS, K * BS)
    entries = 0.012 * jax.random.normal(jax.random.fold_in(key, 22), shape_full, jnp.float32)
    diag_vals = jnp.exp(jax.random.uniform(jax.random.fold_in(key, 23), (NB_TOTAL, BS), jnp.float32, 0.0, math.log(4.0)))
    identity = (jnp.arange(BS)[:, None] == jnp.arange(K * BS)[None, :]).astype(jnp.float32)
    return (entries + identity[None, :, :] * diag_vals[:, :, None]).astype(jnp.bfloat16)


def set_ends(array, key, smallest, largest):
    longest = array.shape.index(max(array.shape))
    spots = []
    for shift in (0, 1):
        where = [jax.random.randint(jax.random.fold_in(key, axis), (), 0, length) for axis, length in enumerate(array.shape)]
        where[longest] = (where[longest] + shift) % array.shape[longest]
        spots.append(tuple(where))
    return array.at[spots[0]].set(smallest).at[spots[1]].set(largest)


def level_of(stream_key, dims, pieces, low, top_value):
    level, own = 1.0, jax.random.fold_in(stream_key, 6)
    for dim, shards_of in pieces:
        draws = jnp.exp(jax.random.uniform(jax.random.fold_in(own, dim), (shards_of,), jnp.float32, low / len(pieces), top_value / len(pieces)))
        level = level * jnp.repeat(draws, dims[dim] // shards_of).reshape([-1 if axis == dim else 1 for axis in range(len(dims))])
    return level


def shared_out(stream_key, own, number, rows, count, top, most, skew):
    order = jax.random.permutation(stream_key, count)
    heavy_load, common = load_shares(count, rows * top, most, skew, True), load_shares(count, rows * top, most, skew, False)
    places = jnp.arange(count)

    def named(lengths, turn):
        used = int((lengths > 0).sum())
        fixed = max(1, used // 4)
        moved = fixed + (places - fixed + turn * (used - fixed)) % max(1, count - fixed)
        return jnp.zeros((count,), jnp.int32).at[order[jnp.where(places < fixed, places, moved)]].set(jnp.asarray(lengths, jnp.int32))

    lengths = jnp.where(number % 4 == 0, named(heavy_load, number // 4), named(common, number - number // 4 - 1))
    mixed = jax.random.permutation(jax.random.fold_in(own, 3), count)
    donor, taker = mixed[0:count // 2 * 2:2], mixed[1:count // 2 * 2:2]
    margin = jnp.minimum(lengths[donor] - 1, most - lengths[taker]) // 2
    margin = jnp.where((donor == order[0]) | (taker == order[0]) | (lengths[taker] == 0), 0, jnp.maximum(margin, 0))
    moved = jax.random.randint(jax.random.fold_in(own, 4), (count // 2,), 0, 1 << 20) % (margin + 1)
    lengths = lengths.at[donor].add(-moved).at[taker].add(moved)
    labels = jnp.searchsorted(jnp.cumsum(lengths), jnp.arange(rows * top), side="right").astype(jnp.int32)
    table = labels.reshape(top, rows).T
    table = table[jax.random.permutation(jax.random.fold_in(own, 1), rows)]
    turn = jax.random.randint(jax.random.fold_in(own, 2), (rows, 1), 0, top)
    return jnp.take_along_axis(table, (jnp.arange(top)[None, :] + turn) % top, axis=1)


def load_shares(amount, total, most, skew, full):
    loads = [(1 << 20) // math.isqrt(grade ** skew) + 1 for grade in range(1, amount + 1)]
    largest = most if full else min(most, max(-(-total // amount), total * loads[0] // sum(loads)))
    least = 1 if total - largest >= amount - 1 else 0
    given, spare = [largest] + [least] * (amount - 1), total - largest - least * (amount - 1)
    while spare > 0:
        movable = [i for i in range(1, amount) if given[i] < largest] or [i for i in range(1, amount) if given[i] < most]
        whole, budget = sum([loads[i] for i in movable]), spare
        for i in movable:
            addition = min(most - given[i], max(1, budget * loads[i] // whole), spare)
            given[i] = given[i] + addition
            spare = spare - addition
    return np.array(given)


def gaussian(key, shape, width, reach, pieces=(), kind=jnp.bfloat16):
    drawn = width * jax.random.normal(key, shape, jnp.float32)
    if pieces:
        drawn = drawn * level_of(key, shape, pieces, -0.22, 0.18)
    return jnp.clip(drawn, -reach, reach).astype(kind)


def setup_inputs(seed: int = 0) -> dict:
    keys = jax.random.split(jax.random.key(seed), 10)
    current = gaussian(keys[0], (E_TOTAL, W), 1.0, 6.0, ((0, 256),))
    resistivity = jnp.clip(jnp.exp(math.log(4.0) - 2.0794415 * jax.random.uniform(keys[1], (E_TOTAL,), jnp.float32) ** level_of(keys[1], (E_TOTAL,), ((0, 256),), -0.2, 0.2)), 0.5, 4.0).astype(jnp.bfloat16)
    temp_coef = jnp.clip(jnp.exp(math.log(0.5) - 1.6133518 * jax.random.uniform(keys[2], (E_TOTAL,), jnp.float32) ** level_of(keys[2], (E_TOTAL,), ((0, 256),), -0.2, 0.2)), 0.099609375, 0.5).astype(jnp.bfloat16)
    dest_part_keys = jax.random.split(jax.random.fold_in(keys[3], 1), E_TOTAL // E_DEV)
    dest_part_turns = jax.random.permutation(jax.random.fold_in(keys[3], 3), E_TOTAL // E_DEV)
    dest_part = jax.vmap(lambda own, number: shared_out(jax.random.fold_in(keys[3], 2), own, number, E_DEV, N_DOM, 1, CAP, 2))(dest_part_keys, dest_part_turns).reshape((E_TOTAL, 1))
    dest_row = set_ends(jax.random.randint(keys[4], (E_TOTAL,), 0, NODES_DEV), jax.random.fold_in(keys[4], 1), 0, NODES_DEV - 1).astype(jnp.int32)
    temp_old = gaussian(keys[5], (NODES, W), 1.0, 6.0, ((0, 256),), jnp.float32)
    heat_cap = jnp.clip(jnp.exp(math.log(2.0) - 2.0794415 * jax.random.uniform(keys[6], (NODES,), jnp.float32) ** level_of(keys[6], (NODES,), ((0, 256),), -0.2, 0.2)), 0.25, 2.0)
    conduction = draw_conduction(jax.random.fold_in(keys[9], 71), 0)
    block_cols = draw_block_cols(jax.random.fold_in(keys[9], 71), 0)
    return {"current": current, "resistivity": resistivity, "temp_coef": temp_coef, "dest_part": dest_part, "dest_row": dest_row, "temp_old": temp_old, "heat_cap": heat_cap, "conduction": conduction, "block_cols": block_cols}


def reference(current, resistivity, temp_coef, dest_part, dest_row, temp_old, heat_cap, conduction, block_cols):
    em_total = current.shape[0]
    element_ids = jnp.arange(em_total, dtype=jnp.int32)
    blk_index = (element_ids // E_DEV) % N_BLK
    node_index = (dest_part[:, 0] * N_BLK + blk_index) * NODES_DEV + dest_row
    current_wide = current.astype(jnp.float32)
    resist_wide = resistivity.astype(jnp.float32)
    power_loss = resist_wide[:, None] * current_wide * current_wide
    node_total = temp_old.shape[0]
    heat_source = jax.ops.segment_sum(power_loss, node_index, num_segments=node_total)
    right_side = heat_cap[:, None] * temp_old + heat_source
    block_total = conduction.shape[0]
    diag_cond = jnp.diagonal(conduction[:, :, :BS], axis1=1, axis2=2).reshape(-1).astype(jnp.float32)
    pivot_sum = heat_cap + diag_cond
    field_now = temp_old
    for sweep_idx in range(SWEEPS):
        field_low = field_now.astype(jnp.bfloat16).reshape(block_total, BS, W)
        applied = jnp.zeros((block_total, BS, W), jnp.float32)
        for slot_idx in range(K):
            picked = field_low[block_cols[:, slot_idx]].astype(jnp.float32)
            block_slice = conduction[:, :, slot_idx * BS:(slot_idx + 1) * BS].astype(jnp.float32)
            applied = applied + jnp.einsum("rij,rjw->riw", block_slice, picked)
        applied = applied.reshape(node_total, W)
        field_now = field_now + (right_side - heat_cap[:, None] * field_now - applied) / pivot_sum[:, None]
    node_temps = field_now[node_index]
    coef_wide = temp_coef.astype(jnp.float32)
    resist_new = (resist_wide[:, None] * (1.0 + coef_wide[:, None] * node_temps)).astype(jnp.bfloat16)
    return field_now, resist_new
```

```python
import jax
import jax.numpy as jnp
from jax import lax
from jax.experimental import pallas as pl
from jax.experimental.pallas import tpu as pltpu
from jax.sharding import PartitionSpec as P

HB = 12
CAP = 128
META = 8
LANES = 128
F32 = jnp.float32
BF16 = jnp.bfloat16
VMEM = pl.BlockSpec(memory_space=pltpu.VMEM)
SMEM = pl.BlockSpec(memory_space=pltpu.SMEM)
PARAMS = pltpu.CompilerParams(vmem_limit_bytes=56 * 1024 * 1024)


def dot(a, b):
    return jnp.dot(a, b, preferred_element_type=F32)


def iota(shape, dim):
    return lax.broadcasted_iota(jnp.int32, shape, dim)


def pack_kernel(part_ref, row_ref, res_ref, coef_ref, cur_ref, send_ref, slot_ref, slot_vmem, wide, spread, sem):
    peers = send_ref.shape[0]
    chunks = part_ref.shape[0]
    before = (iota((LANES, LANES), 0) < iota((LANES, LANES), 1)).astype(BF16)
    counter = jnp.concatenate([before, jnp.ones((LANES, LANES), BF16)], axis=1)
    carry = jnp.zeros((peers, LANES), F32)
    meta = jnp.zeros((4 * peers, LANES), F32)
    part = part_ref[...]
    row = row_ref[...]
    high = lax.shift_right_logical(row, 7).astype(F32)
    low = jnp.bitwise_and(row, 127).astype(F32)
    res = res_ref[...].astype(F32)
    coef = coef_ref[...].astype(F32)
    slots = []
    for r in range(chunks):
        hit = (iota((peers, LANES), 0) == part[r : r + 1]).astype(F32)
        counted = dot(hit.astype(BF16), counter)
        rank = jnp.sum(hit * (counted[:, :LANES] + carry), axis=0, keepdims=True)
        carry = carry + counted[:, LANES:]
        rank = rank.astype(jnp.int32)
        slots.append(part[r : r + 1] * CAP + rank)
        place = (iota((CAP, LANES), 0) == rank).astype(F32).astype(BF16)
        values = jnp.concatenate(
            [hit * res[r : r + 1], hit * coef[r : r + 1], hit * high[r : r + 1], hit * low[r : r + 1]], axis=0
        ).astype(BF16)
        meta = meta + lax.dot_general(values, place, (((1,), (1,)), ((), ())), preferred_element_type=F32)
    slot_vmem[...] = jnp.concatenate(slots, axis=0)
    copy = pltpu.make_async_copy(slot_vmem, slot_ref, sem)
    copy.start()
    wide[...] = cur_ref[...].astype(F32)
    spread[...] = jnp.zeros(spread.shape, F32)
    copy.wait()

    def scatter(r, carry):
        for lane in range(LANES):
            spread[pl.ds(slot_ref[r, lane], 1), :] = wide[pl.ds(r * LANES + lane, 1), :]
        return carry

    lax.fori_loop(0, chunks, scatter, 0)
    for p in range(peers):
        send_ref[p, :CAP] = spread[p * CAP : (p + 1) * CAP].astype(BF16)
    rows = [meta[i * peers : (i + 1) * peers] for i in range(4)]
    for p in range(peers):
        own = jnp.concatenate([m[p : p + 1] for m in rows] + [jnp.zeros((META - 4, LANES), F32)], axis=0)
        send_ref[p, CAP:] = own.astype(BF16)


def pack(part, row, res, coef, cur, peers):
    count, samples = cur.shape
    chunks = count // LANES
    return pl.pallas_call(
        pack_kernel,
        out_shape=(
            jax.ShapeDtypeStruct((peers, CAP + META, samples), BF16),
            jax.ShapeDtypeStruct((chunks, LANES), jnp.int32),
        ),
        in_specs=[VMEM] * 5,
        out_specs=(VMEM, SMEM),
        scratch_shapes=[
            pltpu.VMEM((chunks, LANES), jnp.int32),
            pltpu.VMEM((count, samples), F32),
            pltpu.VMEM((peers * CAP, samples), F32),
            pltpu.SemaphoreType.DMA,
        ],
        compiler_params=PARAMS,
        name="pack",
    )(part, row, res, coef, cur)


def apply_blocks(cols_ref, cond_ref, window_ref, r):
    size = cond_ref.shape[1]
    picked = []
    for k in range(cols_ref.shape[1]):
        start = pl.multiple_of(cols_ref[r, k] * size, size)
        picked.append(window_ref[pl.ds(start, size), :])
    return dot(cond_ref[r], jnp.concatenate(picked, axis=0))


def first_kernel(cols_ref, cond_ref, window_ref, cap_ref, applied_ref, pivot_ref):
    blocks, size, _ = cond_ref.shape
    samples = window_ref.shape[1]
    eye = iota((size, size), 0) == iota((size, size), 1)

    def step(r, carry):
        rows = pl.ds(pl.multiple_of(r * size, size), size)
        applied_ref[rows, :] = apply_blocks(cols_ref, cond_ref, window_ref, r)
        corner = cond_ref[r, :, :size].astype(F32)
        diag = jnp.sum(jnp.where(eye, corner, 0.0), axis=1, keepdims=True)
        pivot = diag + cap_ref[rows, :]
        pivot_ref[rows, :] = jnp.broadcast_to(1.0 / pivot, (size, samples))
        return carry

    lax.fori_loop(0, blocks, step, 0, unroll=2)


def first_sweep(cols, cond, window, cap):
    nodes = cond.shape[0] * cond.shape[1]
    samples = window.shape[1]
    return pl.pallas_call(
        first_kernel,
        out_shape=(jax.ShapeDtypeStruct((nodes, samples), F32),) * 2,
        in_specs=[SMEM, VMEM, VMEM, VMEM],
        out_specs=(VMEM, VMEM),
        compiler_params=PARAMS,
        cost_estimate=pl.CostEstimate(flops=8_000_000_000, bytes_accessed=8_000_000, transcendentals=0),
        name="first_sweep",
    )(cols, cond, window, cap)


GROUP = 8


def gather_kernel(recv_ref, old_ref, cap_ref, applied_ref, pivot_ref, field_ref, right_ref, low_ref, chosen, values, total):
    peers = recv_ref.shape[0]
    nodes, samples = old_ref.shape
    tiles = nodes // LANES
    sub = iota((LANES, LANES), 0).astype(F32)
    total[...] = jnp.zeros(total.shape, F32)

    def step(g, carry):
        for j in range(GROUP):
            p = g * GROUP + j
            cur = recv_ref[p, :CAP].astype(F32)
            square = cur * cur
            top = square.astype(BF16)
            rest = (square - top.astype(F32)).astype(BF16)
            values[j * CAP : (j + 1) * CAP, :] = jnp.concatenate([top, rest], axis=1)
            meta = recv_ref[p, CAP:].astype(F32)
            low_hit = jnp.where(sub == meta[3:4], meta[0:1], 0.0).astype(BF16)
            for t in range(tiles):
                high_hit = jnp.where(meta[2:3] == float(t), 1.0, 0.0)
                high_hit = jnp.broadcast_to(high_hit, (LANES, CAP)).astype(BF16)
                chosen[t * LANES : (t + 1) * LANES, j * CAP : (j + 1) * CAP] = low_hit * high_hit
        total[...] += dot(chosen[...], values[...])
        return carry

    lax.fori_loop(0, peers // GROUP, step, 0)
    heat = total[:, :samples] + total[:, samples:]
    old = old_ref[...]
    field = old + (heat - applied_ref[...]) * pivot_ref[...]
    field_ref[...] = field
    right_ref[...] = cap_ref[...] * old + heat
    low_ref[...] = field.astype(BF16)


def gather_heat(recv, old, cap, applied, pivot):
    nodes, samples = old.shape
    return pl.pallas_call(
        gather_kernel,
        out_shape=(
            jax.ShapeDtypeStruct((nodes, samples), F32),
            jax.ShapeDtypeStruct((nodes, samples), F32),
            jax.ShapeDtypeStruct((nodes, samples), BF16),
        ),
        in_specs=[VMEM] * 5,
        out_specs=(VMEM,) * 3,
        scratch_shapes=[
            pltpu.VMEM((nodes, GROUP * CAP), BF16),
            pltpu.VMEM((GROUP * CAP, 2 * samples), BF16),
            pltpu.VMEM((nodes, 2 * samples), F32),
        ],
        compiler_params=PARAMS,
        name="gather_heat",
    )(recv, old, cap, applied, pivot)


def last_kernel(cols_ref, cond_ref, window_ref, cap_ref, pivot_ref, field_ref, right_ref, recv_ref, temp_ref, back_ref, pair, columns):
    blocks, size, _ = cond_ref.shape
    nodes, samples = field_ref.shape
    peers = recv_ref.shape[0]
    tiles = nodes // LANES

    def step(r, carry):
        rows = pl.ds(pl.multiple_of(r * size, size), size)
        applied = apply_blocks(cols_ref, cond_ref, window_ref, r)
        field = field_ref[rows, :]
        temp = field + (right_ref[rows, :] - cap_ref[rows, :] * field - applied) * pivot_ref[rows, :]
        temp_ref[rows, :] = temp
        top = temp.astype(BF16)
        rest = (temp - top.astype(F32)).astype(BF16)
        pair[rows, :] = jnp.concatenate([top, rest], axis=1)
        return carry

    lax.fori_loop(0, blocks, step, 0, unroll=2)
    for g in range(peers // 16):
        stacked = jnp.concatenate([recv_ref[g * 16 + j, CAP:].astype(F32) for j in range(16)], axis=0)
        columns[g] = stacked.T
    lane = iota((CAP, LANES), 1).astype(F32)

    def send(g, carry):
        for j in range(16):
            own = columns[g, :, j * META : j * META + 4]
            low = jnp.broadcast_to(own[:, 3:4], (CAP, LANES))
            low_hit = jnp.where(low == lane, 1.0, 0.0).astype(BF16)
            high = jnp.broadcast_to(own[:, 2:3], (CAP, LANES))
            hits = [low_hit * jnp.where(high == float(t), 1.0, 0.0).astype(BF16) for t in range(tiles)]
            both = dot(jnp.concatenate(hits, axis=1), pair[...])
            seen = both[:, :samples] + both[:, samples:]
            back_ref[g * 16 + j] = (own[:, 0:1] * (1.0 + own[:, 1:2] * seen)).astype(BF16)
        return carry

    lax.fori_loop(0, peers // 16, send, 0)


def last_sweep(cols, cond, window, cap, pivot, field, right, recv):
    nodes, samples = field.shape
    peers = recv.shape[0]
    return pl.pallas_call(
        last_kernel,
        out_shape=(
            jax.ShapeDtypeStruct((nodes, samples), F32),
            jax.ShapeDtypeStruct((peers, CAP, samples), BF16),
        ),
        in_specs=[SMEM] + [VMEM] * 7,
        out_specs=(VMEM, VMEM),
        scratch_shapes=[
            pltpu.VMEM((nodes, 2 * samples), BF16),
            pltpu.VMEM((peers // 16, CAP, LANES), F32),
        ],
        compiler_params=PARAMS,
        name="last_sweep",
    )(cols, cond, window, cap, pivot, field, right, recv)


def unpack_kernel(slot_ref, back_ref, out_ref, wide, picked):
    peers, _, samples = back_ref.shape
    for p in range(peers):
        wide[p * CAP : (p + 1) * CAP] = back_ref[p].astype(F32)

    def gather(r, carry):
        for lane in range(LANES):
            picked[pl.ds(r * LANES + lane, 1), :] = wide[pl.ds(slot_ref[r, lane], 1), :]
        return carry

    lax.fori_loop(0, slot_ref.shape[0], gather, 0)
    out_ref[...] = picked[...].astype(BF16)


def unpack(slots, back):
    peers, _, samples = back.shape
    count = slots.shape[0] * slots.shape[1]
    return pl.pallas_call(
        unpack_kernel,
        out_shape=jax.ShapeDtypeStruct((count, samples), BF16),
        in_specs=[SMEM, VMEM],
        out_specs=VMEM,
        scratch_shapes=[pltpu.VMEM((peers * CAP, samples), F32), pltpu.VMEM((count, samples), F32)],
        compiler_params=PARAMS,
        name="unpack",
    )(slots, back)


def extended(cells, width):
    axes = ("dom", "blk")
    count = lax.axis_size(axes)
    head = cells[:width]
    tail = cells[cells.shape[0] - width :]
    return jnp.concatenate(
        [
            lax.ppermute(tail, axes, [(i, (i + 1) % count) for i in range(count)]),
            cells,
            lax.ppermute(head, axes, [((i + 1) % count, i) for i in range(count)]),
        ],
        axis=0,
    )


def body(current, resistivity, temp_coef, dest_part, dest_row, temp_old, heat_cap, conduction, block_cols):
    count, samples = current.shape
    peers = lax.axis_size("dom")
    blocks, size, _ = conduction.shape
    chunks = count // LANES
    send, slots = pack(
        dest_part.reshape(chunks, LANES),
        dest_row.reshape(chunks, LANES),
        resistivity.reshape(chunks, LANES),
        temp_coef.reshape(chunks, LANES),
        current,
        peers,
    )
    recv = lax.all_to_all(send, "dom", split_axis=0, concat_axis=0, tiled=True)
    devices = lax.axis_size(("dom", "blk"))
    first_block = lax.axis_index(("dom", "blk")) * blocks
    cols = jnp.mod(block_cols - first_block + HB, blocks * devices)
    cap = heat_cap[:, None]
    window = extended(temp_old.astype(BF16), HB * size)
    applied, pivot = first_sweep(cols, conduction, window, cap)
    field, right, low = gather_heat(recv, temp_old, cap, applied, pivot)
    window = extended(low, HB * size)
    temp, back = last_sweep(cols, conduction, window, cap, pivot, field, right, recv)
    returned = lax.all_to_all(back, "dom", split_axis=0, concat_axis=0, tiled=True)
    return temp, unpack(slots, returned)


def solution(mesh):
    both = ("dom", "blk")
    placed = (
        P(both, None),
        P(both),
        P(both),
        P(both, None),
        P(both),
        P(both, None),
        P(both),
        P(both, None, None),
        P(both, None),
    )
    return jax.shard_map(
        body,
        mesh=mesh,
        in_specs=placed,
        out_specs=(P(both, None), P(both, None)),
        check_vma=False,
    )
```

```python
import jax
import jax.numpy as jnp
from jax import lax
from jax.experimental import pallas as pl
from jax.experimental.pallas import tpu as pltpu
from jax.sharding import PartitionSpec as P

HB = 12
CAP = 128
META = 8
LANES = 128
F32 = jnp.float32
BF16 = jnp.bfloat16
VMEM = pl.BlockSpec(memory_space=pltpu.VMEM)
SMEM = pl.BlockSpec(memory_space=pltpu.SMEM)


def params(mib):
    return pltpu.CompilerParams(vmem_limit_bytes=mib * 1024 * 1024)


def dot(a, b):
    return jnp.dot(a, b, preferred_element_type=F32)


def iota(shape, dim):
    return lax.broadcasted_iota(jnp.int32, shape, dim)


def pack_kernel(part_ref, row_ref, res_ref, coef_ref, cur_ref, send_ref, slot_ref, slot_vmem, wide, spread, sem):
    peers = send_ref.shape[0]
    chunks = part_ref.shape[0]
    before = (iota((LANES, LANES), 0) < iota((LANES, LANES), 1)).astype(BF16)
    counter = jnp.concatenate([before, jnp.ones((LANES, LANES), BF16)], axis=1)
    carry = jnp.zeros((peers, LANES), F32)
    meta = jnp.zeros((4 * peers, LANES), F32)
    part = part_ref[...]
    row = row_ref[...]
    high = lax.shift_right_logical(row, 7).astype(F32)
    low = jnp.bitwise_and(row, 127).astype(F32)
    res = res_ref[...].astype(F32)
    coef = coef_ref[...].astype(F32)
    slots = []
    for r in range(chunks):
        hit = (iota((peers, LANES), 0) == part[r : r + 1]).astype(F32)
        counted = dot(hit.astype(BF16), counter)
        rank = jnp.sum(hit * (counted[:, :LANES] + carry), axis=0, keepdims=True)
        carry = carry + counted[:, LANES:]
        rank = rank.astype(jnp.int32)
        slots.append(part[r : r + 1] * CAP + rank)
        place = (iota((CAP, LANES), 0) == rank).astype(F32).astype(BF16)
        values = jnp.concatenate(
            [hit * res[r : r + 1], hit * coef[r : r + 1], hit * high[r : r + 1], hit * low[r : r + 1]], axis=0
        ).astype(BF16)
        meta = meta + lax.dot_general(values, place, (((1,), (1,)), ((), ())), preferred_element_type=F32)
    slot_vmem[...] = jnp.concatenate(slots, axis=0)
    copy = pltpu.make_async_copy(slot_vmem, slot_ref, sem)
    copy.start()
    wide[...] = cur_ref[...].astype(F32)
    spread[...] = jnp.zeros(spread.shape, F32)
    copy.wait()

    def scatter(r, carry):
        for lane in range(LANES):
            spread[pl.ds(slot_ref[r, lane], 1), :] = wide[pl.ds(r * LANES + lane, 1), :]
        return carry

    lax.fori_loop(0, chunks, scatter, 0)
    for p in range(peers):
        send_ref[p, :CAP] = spread[p * CAP : (p + 1) * CAP].astype(BF16)
    rows = [meta[i * peers : (i + 1) * peers] for i in range(4)]
    for p in range(peers):
        own = jnp.concatenate([m[p : p + 1] for m in rows] + [jnp.zeros((META - 4, LANES), F32)], axis=0)
        send_ref[p, CAP:] = own.astype(BF16)


def pack(part, row, res, coef, cur, peers):
    count, samples = cur.shape
    chunks = count // LANES
    return pl.pallas_call(
        pack_kernel,
        out_shape=(
            jax.ShapeDtypeStruct((peers, CAP + META, samples), BF16),
            jax.ShapeDtypeStruct((chunks, LANES), jnp.int32),
        ),
        in_specs=[VMEM] * 5,
        out_specs=(VMEM, SMEM),
        scratch_shapes=[
            pltpu.VMEM((chunks, LANES), jnp.int32),
            pltpu.VMEM((count, samples), F32),
            pltpu.VMEM((peers * CAP, samples), F32),
            pltpu.SemaphoreType.DMA,
        ],
        compiler_params=params(24),
        name="pack",
    )(part, row, res, coef, cur)


def apply_blocks(cols_ref, cond_ref, window_ref, r):
    size = cond_ref.shape[1]
    picked = []
    for k in range(cols_ref.shape[1]):
        start = pl.multiple_of(cols_ref[r, k] * size, size)
        picked.append(window_ref[pl.ds(start, size), :])
    return dot(cond_ref[r], jnp.concatenate(picked, axis=0))


def fill(window_ref, left_ref, own_ref, right_ref):
    width, nodes = left_ref.shape[0], own_ref.shape[0]
    window_ref[:width] = left_ref[...]
    window_ref[width : width + nodes] = own_ref[...].astype(BF16)
    window_ref[width + nodes :] = right_ref[...]


def first_kernel(cols_ref, cond_ref, left_ref, old_ref, right_ref, cap_ref, applied_ref, pivot_ref, window_ref):
    fill(window_ref, left_ref, old_ref, right_ref)
    blocks, size, _ = cond_ref.shape
    samples = window_ref.shape[1]
    eye = iota((size, size), 0) == iota((size, size), 1)

    def step(r, carry):
        rows = pl.ds(pl.multiple_of(r * size, size), size)
        applied_ref[rows, :] = apply_blocks(cols_ref, cond_ref, window_ref, r)
        corner = cond_ref[r, :, :size].astype(F32)
        diag = jnp.sum(jnp.where(eye, corner, 0.0), axis=1, keepdims=True)
        pivot = diag + cap_ref[rows, :]
        pivot_ref[rows, :] = jnp.broadcast_to(1.0 / pivot, (size, samples))
        return carry

    lax.fori_loop(0, blocks, step, 0, unroll=8)


def first_sweep(cols, cond, left, old, right, cap):
    nodes = cond.shape[0] * cond.shape[1]
    samples = old.shape[1]
    return pl.pallas_call(
        first_kernel,
        out_shape=(jax.ShapeDtypeStruct((nodes, samples), F32),) * 2,
        in_specs=[SMEM] + [VMEM] * 5,
        out_specs=(VMEM, VMEM),
        scratch_shapes=[pltpu.VMEM((nodes + 2 * left.shape[0], samples), BF16)],
        compiler_params=params(16),
        cost_estimate=pl.CostEstimate(flops=8_000_000_000, bytes_accessed=8_000_000, transcendentals=0),
        name="first_sweep",
    )(cols, cond, left, old, right, cap)


MT = 4
STEP = 8


def gather_kernel(recv_ref, old_ref, cap_ref, applied_ref, pivot_ref, field_ref, right_ref, low_ref, head_ref, tail_ref, base, high, values):
    peers = recv_ref.shape[0]
    nodes, samples = old_ref.shape
    tiles = nodes // LANES
    outer = head_ref.shape[0] // LANES
    sub = iota((LANES, LANES), 0).astype(F32)

    def split(p, carry):
        rows = pl.ds(pl.multiple_of(p * CAP, CAP), CAP)
        cur = recv_ref[p, :CAP].astype(F32)
        square = cur * cur
        top = square.astype(BF16)
        rest = (square - top.astype(F32)).astype(BF16)
        values[rows, :] = jnp.concatenate([top, rest], axis=1)
        meta = recv_ref[p, CAP:].astype(F32)
        base[:, rows] = jnp.where(sub == meta[3:4], meta[0:1], 0.0).astype(BF16)
        high[:, rows] = jnp.broadcast_to(meta[2:3], (16, CAP)).astype(BF16)
        return carry

    lax.fori_loop(0, peers, split, 0, unroll=4)
    part = peers * CAP // STEP

    def tile(t, carry):
        both = jnp.zeros((MT * LANES, 2 * samples), F32)
        for c in range(STEP):
            cols = slice(c * part, (c + 1) * part)
            own_base = base[:, cols]
            own_high = high[:, cols]
            hits = []
            for i in range(MT):
                own = (t * MT + i).astype(F32).astype(BF16)
                hit = (own_high == own).astype(BF16)
                hits.append(own_base * jnp.concatenate([hit] * (LANES // 16), axis=0))
            both = both + dot(jnp.concatenate(hits, axis=0), values[cols, :])
        rows = pl.ds(pl.multiple_of(t * MT * LANES, LANES), MT * LANES)
        heat = both[:, :samples] + both[:, samples:]
        old = old_ref[rows, :]
        field = old + (heat - applied_ref[rows, :]) * pivot_ref[rows, :]
        field_ref[rows, :] = field
        right_ref[rows, :] = cap_ref[rows, :] * old + heat
        low_ref[rows, :] = field.astype(BF16)
        return carry

    lax.fori_loop(0, tiles // MT, tile, 0)
    head_ref[...] = low_ref[: outer * LANES]
    tail_ref[...] = low_ref[nodes - outer * LANES :]


def gather_heat(recv, old, cap, applied, pivot, width):
    nodes, samples = old.shape
    slots = recv.shape[0] * CAP
    return pl.pallas_call(
        gather_kernel,
        out_shape=(
            jax.ShapeDtypeStruct((nodes, samples), F32),
            jax.ShapeDtypeStruct((nodes, samples), F32),
            jax.ShapeDtypeStruct((nodes, samples), BF16),
            jax.ShapeDtypeStruct((width, samples), BF16),
            jax.ShapeDtypeStruct((width, samples), BF16),
        ),
        in_specs=[VMEM] * 5,
        out_specs=(VMEM,) * 5,
        scratch_shapes=[
            pltpu.VMEM((LANES, slots), BF16),
            pltpu.VMEM((16, slots), BF16),
            pltpu.VMEM((slots, 2 * samples), BF16),
        ],
        compiler_params=params(24),
        name="gather_heat",
    )(recv, old, cap, applied, pivot)


def last_kernel(cols_ref, cond_ref, left_ref, low_ref, next_ref, cap_ref, pivot_ref, field_ref, right_ref, meta_ref, temp_ref, back_ref, window_ref, pair, columns):
    fill(window_ref, left_ref, low_ref, next_ref)
    blocks, size, _ = cond_ref.shape
    nodes, samples = field_ref.shape
    peers = meta_ref.shape[0]
    tiles = nodes // LANES

    def step(r, carry):
        rows = pl.ds(pl.multiple_of(r * size, size), size)
        applied = apply_blocks(cols_ref, cond_ref, window_ref, r)
        field = field_ref[rows, :]
        temp = field + (right_ref[rows, :] - cap_ref[rows, :] * field - applied) * pivot_ref[rows, :]
        temp_ref[rows, :] = temp
        top = temp.astype(BF16)
        rest = (temp - top.astype(F32)).astype(BF16)
        pair[rows, :] = jnp.concatenate([top, rest], axis=1)
        return carry

    lax.fori_loop(0, blocks, step, 0, unroll=8)
    for g in range(peers // 16):
        stacked = jnp.concatenate([meta_ref[g * 16 + j].astype(F32) for j in range(16)], axis=0)
        columns[g] = stacked.T
    lane = iota((CAP, LANES), 1).astype(F32)

    def send(g, carry):
        for j in range(16):
            own = columns[g, :, j * META : j * META + 4]
            low = jnp.broadcast_to(own[:, 3:4], (CAP, LANES))
            low_hit = jnp.where(low == lane, 1.0, 0.0).astype(BF16)
            high = jnp.broadcast_to(own[:, 2:3], (CAP, LANES))
            hits = [low_hit * jnp.where(high == float(t), 1.0, 0.0).astype(BF16) for t in range(tiles)]
            both = dot(jnp.concatenate(hits, axis=1), pair[...])
            seen = both[:, :samples] + both[:, samples:]
            back_ref[g * 16 + j] = (own[:, 0:1] * (1.0 + own[:, 1:2] * seen)).astype(BF16)
        return carry

    lax.fori_loop(0, peers // 16, send, 0)


def last_sweep(cols, cond, left, low, next, cap, pivot, field, right, meta):
    nodes, samples = field.shape
    peers = meta.shape[0]
    return pl.pallas_call(
        last_kernel,
        out_shape=(
            jax.ShapeDtypeStruct((nodes, samples), F32),
            jax.ShapeDtypeStruct((peers, CAP, samples), BF16),
        ),
        in_specs=[SMEM] + [VMEM] * 9,
        out_specs=(VMEM, VMEM),
        scratch_shapes=[
            pltpu.VMEM((nodes + 2 * left.shape[0], samples), BF16),
            pltpu.VMEM((nodes, 2 * samples), BF16),
            pltpu.VMEM((peers // 16, CAP, LANES), F32),
        ],
        compiler_params=params(24),
        name="last_sweep",
    )(cols, cond, left, low, next, cap, pivot, field, right, meta)


def unpack_kernel(slot_ref, back_ref, out_ref, wide, picked):
    peers, _, samples = back_ref.shape
    for p in range(peers):
        wide[p * CAP : (p + 1) * CAP] = back_ref[p].astype(F32)

    def gather(r, carry):
        for lane in range(LANES):
            picked[pl.ds(r * LANES + lane, 1), :] = wide[pl.ds(slot_ref[r, lane], 1), :]
        return carry

    lax.fori_loop(0, slot_ref.shape[0], gather, 0)
    out_ref[...] = picked[...].astype(BF16)


def unpack(slots, back):
    peers, _, samples = back.shape
    count = slots.shape[0] * slots.shape[1]
    return pl.pallas_call(
        unpack_kernel,
        out_shape=jax.ShapeDtypeStruct((count, samples), BF16),
        in_specs=[SMEM, VMEM],
        out_specs=VMEM,
        scratch_shapes=[pltpu.VMEM((peers * CAP, samples), F32), pltpu.VMEM((count, samples), F32)],
        compiler_params=params(24),
        name="unpack",
    )(slots, back)


def halo(head, tail):
    axes = ("dom", "blk")
    count = lax.axis_size(axes)
    left = lax.ppermute(tail, axes, [(i, (i + 1) % count) for i in range(count)])
    right = lax.ppermute(head, axes, [((i + 1) % count, i) for i in range(count)])
    return left, right


def body(current, resistivity, temp_coef, dest_part, dest_row, temp_old, heat_cap, conduction, block_cols):
    count, samples = current.shape
    peers = lax.axis_size("dom")
    blocks, size, _ = conduction.shape
    chunks = count // LANES
    width = HB * size
    left, right = halo(temp_old[:width].astype(BF16), temp_old[-width:].astype(BF16))
    send, slots = pack(
        dest_part.reshape(chunks, LANES),
        dest_row.reshape(chunks, LANES),
        resistivity.reshape(chunks, LANES),
        temp_coef.reshape(chunks, LANES),
        current,
        peers,
    )
    send, left, right = lax.optimization_barrier((send, left, right))
    recv = lax.all_to_all(send, "dom", split_axis=0, concat_axis=0, tiled=True)
    devices = lax.axis_size(("dom", "blk"))
    first_block = lax.axis_index(("dom", "blk")) * blocks
    cols = jnp.mod(block_cols - first_block + HB, blocks * devices)
    cap = heat_cap[:, None]
    applied, pivot = first_sweep(cols, conduction, left, temp_old, right, cap)
    field, total, low, head, tail = gather_heat(recv, temp_old, cap, applied, pivot, width)
    left, right = halo(head, tail)
    temp, back = last_sweep(cols, conduction, left, low, right, cap, pivot, field, total, recv[:, CAP:])
    returned = lax.all_to_all(back, "dom", split_axis=0, concat_axis=0, tiled=True)
    return temp, unpack(slots, returned)


def solution(mesh):
    both = ("dom", "blk")
    placed = (
        P(both, None),
        P(both),
        P(both),
        P(both, None),
        P(both),
        P(both, None),
        P(both),
        P(both, None, None),
        P(both, None),
    )
    return jax.shard_map(
        body,
        mesh=mesh,
        in_specs=placed,
        out_specs=(P(both, None), P(both, None)),
        check_vma=False,
    )
```

```python
import jax
import jax.numpy as jnp
from jax import lax
from jax.experimental import pallas as pl
from jax.experimental.pallas import tpu as pltpu
from jax.sharding import PartitionSpec as P

HB = 12
CAP = 128
META = 8
PARTS = 4
LANES = 128
F32 = jnp.float32
BF16 = jnp.bfloat16
VMEM = pl.BlockSpec(memory_space=pltpu.VMEM)
SMEM = pl.BlockSpec(memory_space=pltpu.SMEM)
HBM = pl.BlockSpec(memory_space=pltpu.HBM)


def params(mib):
    return pltpu.CompilerParams(vmem_limit_bytes=mib * 1024 * 1024)


def dot(a, b):
    return jnp.dot(a, b, preferred_element_type=F32)


def iota(shape, dim):
    return lax.broadcasted_iota(jnp.int32, shape, dim)


def pack_kernel(part_ref, row_ref, res_ref, coef_ref, cur_hbm, send_ref, slot_ref, slot_vmem, cur, wide, spread, ready, sem, out_sems):
    peers = send_ref.shape[0]
    fetch = pltpu.make_async_copy(cur_hbm, cur, sem.at[0])
    fetch.start()
    chunks = part_ref.shape[0]
    before = (iota((LANES, LANES), 0) < iota((LANES, LANES), 1)).astype(BF16)
    counter = jnp.concatenate([before, jnp.ones((LANES, LANES), BF16)], axis=1)
    carry = jnp.zeros((peers, LANES), F32)
    meta = jnp.zeros((4 * peers, LANES), F32)
    part = part_ref[...]
    row = row_ref[...]
    high = lax.shift_right_logical(row, 7).astype(F32)
    low = jnp.bitwise_and(row, 127).astype(F32)
    res = res_ref[...].astype(F32)
    coef = coef_ref[...].astype(F32)
    slots = []
    for r in range(chunks):
        hit = (iota((peers, LANES), 0) == part[r : r + 1]).astype(F32)
        counted = dot(hit.astype(BF16), counter)
        rank = jnp.sum(hit * (counted[:, :LANES] + carry), axis=0, keepdims=True)
        carry = carry + counted[:, LANES:]
        rank = rank.astype(jnp.int32)
        slots.append(part[r : r + 1] * CAP + rank)
        place = (iota((CAP, LANES), 0) == rank).astype(F32).astype(BF16)
        values = jnp.concatenate(
            [hit * res[r : r + 1], hit * coef[r : r + 1], hit * high[r : r + 1], hit * low[r : r + 1]], axis=0
        ).astype(BF16)
        meta = meta + lax.dot_general(values, place, (((1,), (1,)), ((), ())), preferred_element_type=F32)
    slot_vmem[...] = jnp.concatenate(slots, axis=0)
    copy = pltpu.make_async_copy(slot_vmem, slot_ref, sem.at[1])
    copy.start()
    spread[...] = jnp.zeros(spread.shape, F32)
    fetch.wait()
    wide[...] = cur[...].astype(F32)
    copy.wait()

    def scatter(r, carry):
        for lane in range(LANES):
            spread[pl.ds(slot_ref[r, lane], 1), :] = wide[pl.ds(r * LANES + lane, 1), :]
        return carry

    lax.fori_loop(0, chunks, scatter, 0)
    rows = [meta[i * peers : (i + 1) * peers] for i in range(4)]
    group = peers // PARTS
    copies = []
    for g in range(PARTS):
        for p in range(g * group, (g + 1) * group):
            own = jnp.concatenate([m[p : p + 1] for m in rows] + [jnp.zeros((META - 4, LANES), F32)], axis=0)
            ready[p, :CAP] = spread[p * CAP : (p + 1) * CAP].astype(BF16)
            ready[p, CAP:] = own.astype(BF16)
        span = pl.ds(g * group, group)
        copies.append(pltpu.make_async_copy(ready.at[span], send_ref.at[span], out_sems.at[g]))
        copies[g].start()
    for copy in copies:
        copy.wait()


def pack(part, row, res, coef, cur, peers):
    count, samples = cur.shape
    chunks = count // LANES
    return pl.pallas_call(
        pack_kernel,
        out_shape=(
            jax.ShapeDtypeStruct((peers, CAP + META, samples), BF16),
            jax.ShapeDtypeStruct((chunks, LANES), jnp.int32),
        ),
        in_specs=[VMEM] * 4 + [HBM],
        out_specs=(HBM, SMEM),
        scratch_shapes=[
            pltpu.VMEM((chunks, LANES), jnp.int32),
            pltpu.VMEM((count, samples), BF16),
            pltpu.VMEM((count, samples), F32),
            pltpu.VMEM((peers * CAP, samples), F32),
            pltpu.VMEM((peers, CAP + META, samples), BF16),
            pltpu.SemaphoreType.DMA((2,)),
            pltpu.SemaphoreType.DMA((PARTS,)),
        ],
        compiler_params=params(60),
        cost_estimate=pl.CostEstimate(flops=8_000_000_000, bytes_accessed=4_000_000, transcendentals=0),
        name="pack",
    )(part, row, res, coef, cur)


def apply_blocks(cols_ref, cond_ref, window_ref, r):
    size = cond_ref.shape[1]
    picked = []
    for k in range(cols_ref.shape[1]):
        start = pl.multiple_of(cols_ref[r, k] * size, size)
        picked.append(window_ref[pl.ds(start, size), :])
    return dot(cond_ref[r], jnp.concatenate(picked, axis=0))


def fill(window_ref, left_ref, own_ref, right_ref):
    width, nodes = left_ref.shape[0], own_ref.shape[0]
    window_ref[:width] = left_ref[...]
    window_ref[width : width + nodes] = own_ref[...].astype(BF16)
    window_ref[width + nodes :] = right_ref[...]


def first_kernel(cols_ref, cond_ref, left_ref, old_ref, right_ref, cap_ref, base_ref, gain_ref, next_ref, slope_ref, window_ref):
    fill(window_ref, left_ref, old_ref, right_ref)
    blocks, size, _ = cond_ref.shape
    samples = window_ref.shape[1]
    eye = iota((size, size), 0) == iota((size, size), 1)

    def step(r, carry):
        rows = pl.ds(pl.multiple_of(r * size, size), size)
        applied = apply_blocks(cols_ref, cond_ref, window_ref, r)
        corner = cond_ref[r, :, :size].astype(F32)
        diag = jnp.sum(jnp.where(eye, corner, 0.0), axis=1, keepdims=True)
        cap = cap_ref[rows, :]
        gain = jnp.broadcast_to(1.0 / (diag + cap), (size, samples))
        cap = jnp.broadcast_to(cap, (size, samples))
        old = old_ref[rows, :]
        base = old - applied * gain
        share = cap * gain
        base_ref[rows, :] = base
        gain_ref[rows, :] = gain
        next_ref[rows, :] = base * (1.0 - share) + share * old
        slope_ref[rows, :] = gain * (2.0 - share)
        return carry

    lax.fori_loop(0, blocks, step, 0, unroll=8)


def first_sweep(cols, cond, left, old, right, cap):
    nodes, samples = old.shape
    return pl.pallas_call(
        first_kernel,
        out_shape=(jax.ShapeDtypeStruct((nodes, samples), F32),) * 4,
        in_specs=[SMEM] + [VMEM] * 5,
        out_specs=(VMEM,) * 4,
        scratch_shapes=[pltpu.VMEM((nodes + 2 * left.shape[0], samples), BF16)],
        compiler_params=params(48),
        cost_estimate=pl.CostEstimate(flops=8_000_000_000, bytes_accessed=8_000_000, transcendentals=0),
        name="first_sweep",
    )(cols, cond, left, old, right, cap)


MT = 4
STEP = 8


def gather_kernel(recv_hbm, base_hbm, gain_hbm, next_hbm, slope_hbm, next_ref, low_ref, head_ref, tail_ref, recv_ref, node_in, chosen, high, values, recv_sems, sems):
    peers = recv_ref.shape[0]
    group = peers // PARTS
    arrivals = []
    for g in range(PARTS):
        span = pl.ds(g * group, group)
        arrivals.append(pltpu.make_async_copy(recv_hbm.at[span], recv_ref.at[span], recv_sems.at[g]))
        arrivals[g].start()
    nodes, samples = next_ref.shape
    tiles = nodes // LANES
    outer = head_ref.shape[0] // LANES
    sources = (base_hbm, gain_hbm, next_hbm, slope_hbm)
    copies = [pltpu.make_async_copy(ref, node_in.at[i], sems.at[i]) for i, ref in enumerate(sources)]
    for copy in copies:
        copy.start()
    sub = iota((LANES, LANES), 0).astype(F32)

    def split(p, carry):
        rows = pl.ds(pl.multiple_of(p * CAP, CAP), CAP)
        cur = recv_ref[p, :CAP].astype(F32)
        square = cur * cur
        top = square.astype(BF16)
        rest = (square - top.astype(F32)).astype(BF16)
        values[rows, :] = jnp.concatenate([top, rest], axis=1)
        meta = recv_ref[p, CAP:].astype(F32)
        chosen[:, rows] = jnp.where(sub == meta[3:4], meta[0:1], 0.0).astype(BF16)
        high[:, rows] = jnp.broadcast_to(meta[2:3], (16, CAP)).astype(BF16)
        return carry

    for g in range(PARTS):
        arrivals[g].wait()
        lax.fori_loop(g * group, (g + 1) * group, split, 0, unroll=4)
    part = peers * CAP // STEP
    for copy in copies:
        copy.wait()

    def tile(t, carry):
        both = jnp.zeros((MT * LANES, 2 * samples), F32)
        for c in range(STEP):
            cols = slice(c * part, (c + 1) * part)
            own_base = chosen[:, cols]
            own_high = high[:, cols]
            hits = []
            for i in range(MT):
                own = (t * MT + i).astype(F32).astype(BF16)
                hit = (own_high == own).astype(BF16)
                hits.append(own_base * jnp.concatenate([hit] * (LANES // 16), axis=0))
            both = both + dot(jnp.concatenate(hits, axis=0), values[cols, :])
        rows = pl.ds(pl.multiple_of(t * MT * LANES, LANES), MT * LANES)
        heat = both[:, :samples] + both[:, samples:]
        field = node_in[0, rows, :] + heat * node_in[1, rows, :]
        next_ref[rows, :] = node_in[2, rows, :] + heat * node_in[3, rows, :]
        low_ref[rows, :] = field.astype(BF16)
        return carry

    lax.fori_loop(0, tiles // MT, tile, 0)
    head_ref[...] = low_ref[: outer * LANES]
    tail_ref[...] = low_ref[nodes - outer * LANES :]


def gather_heat(recv, base, gain, following, slope, width):
    nodes, samples = base.shape
    slots = recv.shape[0] * CAP
    return pl.pallas_call(
        gather_kernel,
        out_shape=(
            jax.ShapeDtypeStruct((nodes, samples), F32),
            jax.ShapeDtypeStruct((nodes, samples), BF16),
            jax.ShapeDtypeStruct((width, samples), BF16),
            jax.ShapeDtypeStruct((width, samples), BF16),
        ),
        in_specs=[HBM] * 5,
        out_specs=(VMEM,) * 4,
        scratch_shapes=[
            pltpu.VMEM(recv.shape, BF16),
            pltpu.VMEM((4, nodes, samples), F32),
            pltpu.VMEM((LANES, slots), BF16),
            pltpu.VMEM((16, slots), BF16),
            pltpu.VMEM((slots, 2 * samples), BF16),
            pltpu.SemaphoreType.DMA((PARTS,)),
            pltpu.SemaphoreType.DMA((4,)),
        ],
        compiler_params=params(52),
        name="gather_heat",
    )(recv, base, gain, following, slope)


def turn_kernel(meta_ref, turned_ref):
    for g in range(meta_ref.shape[0] // 16):
        stacked = jnp.concatenate([meta_ref[g * 16 + j].astype(F32) for j in range(16)], axis=0)
        turned_ref[g] = stacked.T


def turn(meta):
    groups = meta.shape[0] // 16
    return pl.pallas_call(
        turn_kernel,
        out_shape=jax.ShapeDtypeStruct((groups, CAP, LANES), F32),
        in_specs=[VMEM],
        out_specs=VMEM,
        compiler_params=params(8),
        name="turn",
    )(meta)


def last_kernel(cols_ref, cond_ref, left_ref, low_ref, right_ref, next_ref, gain_ref, turned_ref, temp_hbm, back_ref, window_ref, temp, pair, temp_sem):
    fill(window_ref, left_ref, low_ref, right_ref)
    blocks, size, _ = cond_ref.shape
    nodes, samples = next_ref.shape
    groups = turned_ref.shape[0]
    tiles = nodes // LANES

    def step(r, carry):
        rows = pl.ds(pl.multiple_of(r * size, size), size)
        applied = apply_blocks(cols_ref, cond_ref, window_ref, r)
        field = next_ref[rows, :] - applied * gain_ref[rows, :]
        temp[rows, :] = field
        top = field.astype(BF16)
        rest = (field - top.astype(F32)).astype(BF16)
        pair[rows, :] = jnp.concatenate([top, rest], axis=1)
        return carry

    lax.fori_loop(0, blocks, step, 0, unroll=8)
    temp_copy = pltpu.make_async_copy(temp, temp_hbm, temp_sem)
    temp_copy.start()
    lane = iota((CAP, LANES), 1).astype(F32)

    def send(g, carry):
        for j in range(16):
            own = turned_ref[g, :, j * META : j * META + 4]
            low = jnp.broadcast_to(own[:, 3:4], (CAP, LANES))
            low_hit = jnp.where(low == lane, 1.0, 0.0).astype(BF16)
            high = jnp.broadcast_to(own[:, 2:3], (CAP, LANES))
            hits = [low_hit * jnp.where(high == float(t), 1.0, 0.0).astype(BF16) for t in range(tiles)]
            both = dot(jnp.concatenate(hits, axis=1), pair[...])
            seen = both[:, :samples] + both[:, samples:]
            back_ref[g * 16 + j] = (own[:, 0:1] * (1.0 + own[:, 1:2] * seen)).astype(BF16)
        return carry

    lax.fori_loop(0, groups, send, 0)
    temp_copy.wait()


def last_sweep(cols, cond, left, low, right, following, gain, turned):
    nodes, samples = following.shape
    peers = turned.shape[0] * 16
    return pl.pallas_call(
        last_kernel,
        out_shape=(
            jax.ShapeDtypeStruct((nodes, samples), F32),
            jax.ShapeDtypeStruct((peers, CAP, samples), BF16),
        ),
        in_specs=[SMEM] + [VMEM] * 7,
        out_specs=(HBM, VMEM),
        scratch_shapes=[
            pltpu.VMEM((nodes + 2 * left.shape[0], samples), BF16),
            pltpu.VMEM((nodes, samples), F32),
            pltpu.VMEM((nodes, 2 * samples), BF16),
            pltpu.SemaphoreType.DMA,
        ],
        compiler_params=params(24),
        name="last_sweep",
    )(cols, cond, left, low, right, following, gain, turned)


def unpack_kernel(slot_ref, back_ref, out_hbm, wide, picked, out, sems):
    peers, _, samples = back_ref.shape
    for p in range(peers):
        wide[p * CAP : (p + 1) * CAP] = back_ref[p].astype(F32)
    chunks = slot_ref.shape[0] // PARTS

    def gather(r, carry):
        for lane in range(LANES):
            picked[pl.ds(r * LANES + lane, 1), :] = wide[pl.ds(slot_ref[r, lane], 1), :]
        return carry

    copies = []
    for g in range(PARTS):
        lax.fori_loop(g * chunks, (g + 1) * chunks, gather, 0)
        span = pl.ds(g * chunks * LANES, chunks * LANES)
        out[span, :] = picked[span, :].astype(BF16)
        copies.append(pltpu.make_async_copy(out.at[span], out_hbm.at[span], sems.at[g]))
        copies[g].start()
    for copy in copies:
        copy.wait()


def unpack(slots, back):
    peers, _, samples = back.shape
    count = slots.shape[0] * slots.shape[1]
    return pl.pallas_call(
        unpack_kernel,
        out_shape=jax.ShapeDtypeStruct((count, samples), BF16),
        in_specs=[SMEM, VMEM],
        out_specs=HBM,
        scratch_shapes=[
            pltpu.VMEM((peers * CAP, samples), F32),
            pltpu.VMEM((count, samples), F32),
            pltpu.VMEM((count, samples), BF16),
            pltpu.SemaphoreType.DMA((PARTS,)),
        ],
        compiler_params=params(24),
        name="unpack",
    )(slots, back)


def ends_kernel(old_hbm, head_ref, tail_ref, head, tail, sems):
    width, nodes = head.shape[0], old_hbm.shape[0]
    first = pltpu.make_async_copy(old_hbm.at[pl.ds(0, width)], head, sems.at[0])
    last = pltpu.make_async_copy(old_hbm.at[pl.ds(nodes - width, width)], tail, sems.at[1])
    first.start()
    last.start()
    first.wait()
    head_ref[...] = head[...].astype(BF16)
    last.wait()
    tail_ref[...] = tail[...].astype(BF16)


def ends(old, width):
    samples = old.shape[1]
    return pl.pallas_call(
        ends_kernel,
        out_shape=(jax.ShapeDtypeStruct((width, samples), BF16),) * 2,
        in_specs=[HBM],
        out_specs=(VMEM, VMEM),
        scratch_shapes=[
            pltpu.VMEM((width, samples), F32),
            pltpu.VMEM((width, samples), F32),
            pltpu.SemaphoreType.DMA((2,)),
        ],
        compiler_params=params(62),
        name="ends",
    )(old)


def halo(head, tail):
    axes = ("dom", "blk")
    count = lax.axis_size(axes)
    left = lax.ppermute(tail, axes, [(i, (i + 1) % count) for i in range(count)])
    right = lax.ppermute(head, axes, [((i + 1) % count, i) for i in range(count)])
    return left, right


def body(current, resistivity, temp_coef, dest_part, dest_row, temp_old, heat_cap, conduction, block_cols):
    count, samples = current.shape
    peers = lax.axis_size("dom")
    blocks, size, _ = conduction.shape
    chunks = count // LANES
    width = HB * size
    left, right = halo(*ends(temp_old, width))
    send, slots = pack(
        dest_part.reshape(chunks, LANES),
        dest_row.reshape(chunks, LANES),
        resistivity.reshape(chunks, LANES),
        temp_coef.reshape(chunks, LANES),
        current,
        peers,
    )
    send, _, _ = lax.optimization_barrier((send, left, right))
    recv = lax.all_to_all(send, "dom", split_axis=0, concat_axis=0, tiled=True)
    devices = lax.axis_size(("dom", "blk"))
    first_block = lax.axis_index(("dom", "blk")) * blocks
    cols = jnp.mod(block_cols - first_block + HB, blocks * devices)
    base, gain, following, slope = first_sweep(cols, conduction, left, temp_old, right, heat_cap[:, None])
    following, low, head, tail = gather_heat(recv, base, gain, following, slope, width)
    left, right = halo(head, tail)
    temp, back = last_sweep(cols, conduction, left, low, right, following, gain, turn(recv[:, CAP:]))
    returned = lax.all_to_all(back, "dom", split_axis=0, concat_axis=0, tiled=True)
    return temp, unpack(slots, returned)


def solution(mesh):
    both = ("dom", "blk")
    placed = (
        P(both, None),
        P(both),
        P(both),
        P(both, None),
        P(both),
        P(both, None),
        P(both),
        P(both, None, None),
        P(both, None),
    )
    return jax.shard_map(
        body,
        mesh=mesh,
        in_specs=placed,
        out_specs=(P(both, None), P(both, None)),
        check_vma=False,
    )
```

```python
import functools

import jax
import jax.numpy as jnp
from jax import lax
from jax.experimental import pallas as pl
from jax.experimental.pallas import tpu as pltpu
from jax.sharding import PartitionSpec as P

HB = 12
CAP = 128
META = 8
PARTS = 4
LANES = 128
F32 = jnp.float32
BF16 = jnp.bfloat16
VMEM = pl.BlockSpec(memory_space=pltpu.VMEM)
SMEM = pl.BlockSpec(memory_space=pltpu.SMEM)
HBM = pl.BlockSpec(memory_space=pltpu.HBM)


def params(mib):
    return pltpu.CompilerParams(vmem_limit_bytes=mib * 1024 * 1024)


def dot(a, b):
    return jnp.dot(a, b, preferred_element_type=F32)


def iota(shape, dim):
    return lax.broadcasted_iota(jnp.int32, shape, dim)


def pack_kernel(part_ref, row_ref, res_ref, coef_ref, cur_hbm, send_ref, slot_ref, slot_vmem, cur, wide, spread, ready, sem, out_sems):
    peers = send_ref.shape[0]
    fetch = pltpu.make_async_copy(cur_hbm, cur, sem.at[0])
    fetch.start()
    chunks = part_ref.shape[0]
    before = (iota((LANES, LANES), 0) < iota((LANES, LANES), 1)).astype(BF16)
    counter = jnp.concatenate([before, jnp.ones((LANES, LANES), BF16)], axis=1)
    carry = jnp.zeros((peers, LANES), F32)
    meta = jnp.zeros((4 * peers, LANES), F32)
    part = part_ref[...]
    row = row_ref[...]
    high = lax.shift_right_logical(row, 7).astype(F32)
    low = jnp.bitwise_and(row, 127).astype(F32)
    res = res_ref[...].astype(F32)
    coef = coef_ref[...].astype(F32)
    slots = []
    for r in range(chunks):
        hit = (iota((peers, LANES), 0) == part[r : r + 1]).astype(F32)
        counted = dot(hit.astype(BF16), counter)
        rank = jnp.sum(hit * (counted[:, :LANES] + carry), axis=0, keepdims=True)
        carry = carry + counted[:, LANES:]
        rank = rank.astype(jnp.int32)
        slots.append(part[r : r + 1] * CAP + rank)
        place = (iota((CAP, LANES), 0) == rank).astype(F32).astype(BF16)
        values = jnp.concatenate(
            [hit * res[r : r + 1], hit * coef[r : r + 1], hit * high[r : r + 1], hit * low[r : r + 1]], axis=0
        ).astype(BF16)
        meta = meta + lax.dot_general(values, place, (((1,), (1,)), ((), ())), preferred_element_type=F32)
    slot_vmem[...] = jnp.concatenate(slots, axis=0)
    copy = pltpu.make_async_copy(slot_vmem, slot_ref, sem.at[1])
    copy.start()
    spread[...] = jnp.zeros(spread.shape, F32)
    fetch.wait()
    wide[...] = cur[...].astype(F32)
    copy.wait()

    def scatter(r, carry):
        for lane in range(LANES):
            spread[pl.ds(slot_ref[r, lane], 1), :] = wide[pl.ds(r * LANES + lane, 1), :]
        return carry

    lax.fori_loop(0, chunks, scatter, 0)
    rows = [meta[i * peers : (i + 1) * peers] for i in range(4)]
    group = peers // PARTS
    copies = []
    for g in range(PARTS):
        for p in range(g * group, (g + 1) * group):
            own = jnp.concatenate([m[p : p + 1] for m in rows] + [jnp.zeros((META - 4, LANES), F32)], axis=0)
            ready[p, :CAP] = spread[p * CAP : (p + 1) * CAP].astype(BF16)
            ready[p, CAP:] = own.astype(BF16)
        span = pl.ds(g * group, group)
        copies.append(pltpu.make_async_copy(ready.at[span], send_ref.at[span], out_sems.at[g]))
        copies[g].start()
    for copy in copies:
        copy.wait()


def pack(part, row, res, coef, cur, peers):
    count, samples = cur.shape
    chunks = count // LANES
    return pl.pallas_call(
        pack_kernel,
        out_shape=(
            jax.ShapeDtypeStruct((peers, CAP + META, samples), BF16),
            jax.ShapeDtypeStruct((chunks, LANES), jnp.int32),
        ),
        in_specs=[VMEM] * 4 + [HBM],
        out_specs=(HBM, SMEM),
        scratch_shapes=[
            pltpu.VMEM((chunks, LANES), jnp.int32),
            pltpu.VMEM((count, samples), BF16),
            pltpu.VMEM((count, samples), F32),
            pltpu.VMEM((peers * CAP, samples), F32),
            pltpu.VMEM((peers, CAP + META, samples), BF16),
            pltpu.SemaphoreType.DMA((2,)),
            pltpu.SemaphoreType.DMA((PARTS,)),
        ],
        compiler_params=params(60),
        cost_estimate=pl.CostEstimate(flops=8_000_000_000, bytes_accessed=4_000_000, transcendentals=0),
        name="pack",
    )(part, row, res, coef, cur)


def apply_blocks(cols_ref, cond_ref, window_ref, r):
    size = cond_ref.shape[1]
    picked = []
    for k in range(cols_ref.shape[1]):
        start = pl.multiple_of(cols_ref[r, k] * size, size)
        picked.append(window_ref[pl.ds(start, size), :])
    return dot(cond_ref[r], jnp.concatenate(picked, axis=0))


def fill(window_ref, *parts):
    start = 0
    for ref in parts:
        window_ref[start : start + ref.shape[0]] = ref[...].astype(BF16)
        start += ref.shape[0]


def first_kernel(cols_ref, cond_ref, left_ref, old_ref, right_ref, cap_ref, base_ref, gain_ref, next_ref, slope_ref, window_ref):
    fill(window_ref, left_ref, old_ref, right_ref)
    blocks, size, _ = cond_ref.shape
    samples = window_ref.shape[1]
    eye = iota((size, size), 0) == iota((size, size), 1)

    def step(r, carry):
        rows = pl.ds(pl.multiple_of(r * size, size), size)
        applied = apply_blocks(cols_ref, cond_ref, window_ref, r)
        corner = cond_ref[r, :, :size].astype(F32)
        diag = jnp.sum(jnp.where(eye, corner, 0.0), axis=1, keepdims=True)
        cap = cap_ref[rows, :]
        gain = jnp.broadcast_to(1.0 / (diag + cap), (size, samples))
        cap = jnp.broadcast_to(cap, (size, samples))
        old = old_ref[rows, :]
        base = old - applied * gain
        share = cap * gain
        base_ref[rows, :] = base
        gain_ref[rows, :] = gain
        next_ref[rows, :] = base * (1.0 - share) + share * old
        slope_ref[rows, :] = gain * (2.0 - share)
        return carry

    lax.fori_loop(0, blocks, step, 0, unroll=8)


def first_sweep(cols, cond, left, old, right, cap):
    nodes, samples = old.shape
    return pl.pallas_call(
        first_kernel,
        out_shape=(jax.ShapeDtypeStruct((nodes, samples), F32),) * 4,
        in_specs=[SMEM] + [VMEM] * 5,
        out_specs=(VMEM,) * 4,
        scratch_shapes=[pltpu.VMEM((nodes + 2 * left.shape[0], samples), BF16)],
        compiler_params=params(48),
        cost_estimate=pl.CostEstimate(flops=8_000_000_000, bytes_accessed=8_000_000, transcendentals=0),
        name="first_sweep",
    )(cols, cond, left, old, right, cap)


STEP = 8


def gather_kernel(spans, recv_hbm, base_hbm, gain_hbm, next_hbm, slope_hbm, *rest):
    count = len(spans)
    next_refs, low_refs = rest[:count], rest[count : 2 * count]
    recv_ref, node_in, chosen, high, values, recv_sems, sems = rest[2 * count :]
    peers = recv_ref.shape[0]
    group = peers // PARTS
    samples = node_in.shape[2]
    arrivals = []
    for g in range(PARTS):
        span = pl.ds(g * group, group)
        arrivals.append(pltpu.make_async_copy(recv_hbm.at[span], recv_ref.at[span], recv_sems.at[g]))
        arrivals[g].start()
    copies, offsets, offset = [], [], 0
    for k, (first, size) in enumerate(spans):
        for i, ref in enumerate((base_hbm, gain_hbm, next_hbm, slope_hbm)):
            target = node_in.at[i, pl.ds(offset, size)]
            copies.append(pltpu.make_async_copy(ref.at[pl.ds(first, size)], target, sems.at[4 * k + i]))
        offsets.append(offset)
        offset += size
    for copy in copies:
        copy.start()
    sub = iota((LANES, LANES), 0).astype(F32)

    def split(p, carry):
        rows = pl.ds(pl.multiple_of(p * CAP, CAP), CAP)
        cur = recv_ref[p, :CAP].astype(F32)
        square = cur * cur
        top = square.astype(BF16)
        rest = (square - top.astype(F32)).astype(BF16)
        values[rows, :] = jnp.concatenate([top, rest], axis=1)
        meta = recv_ref[p, CAP:].astype(F32)
        chosen[:, rows] = jnp.where(sub == meta[3:4], meta[0:1], 0.0).astype(BF16)
        high[:, rows] = jnp.broadcast_to(meta[2:3], (16, CAP)).astype(BF16)
        return carry

    for g in range(PARTS):
        arrivals[g].wait()
        lax.fori_loop(g * group, (g + 1) * group, split, 0, unroll=4)
    part = peers * CAP // STEP
    for copy in copies:
        copy.wait()
    for k, (first, size) in enumerate(spans):
        mt = next(m for m in (6, 4, 3, 2, 1) if size // LANES % m == 0)

        def tile(t, carry):
            both = jnp.zeros((mt * LANES, 2 * samples), F32)
            for c in range(STEP):
                cols = slice(c * part, (c + 1) * part)
                own_base = chosen[:, cols]
                own_high = high[:, cols]
                hits = []
                for i in range(mt):
                    own = (first // LANES + t * mt + i).astype(F32).astype(BF16)
                    hit = (own_high == own).astype(BF16)
                    hits.append(own_base * jnp.concatenate([hit] * (LANES // 16), axis=0))
                both = both + dot(jnp.concatenate(hits, axis=0), values[cols, :])
            start = pl.multiple_of(t * mt * LANES, LANES)
            rows = pl.ds(start, mt * LANES)
            here = pl.ds(offsets[k] + start, mt * LANES)
            heat = both[:, :samples] + both[:, samples:]
            field = node_in[0, here, :] + heat * node_in[1, here, :]
            next_refs[k][rows, :] = node_in[2, here, :] + heat * node_in[3, here, :]
            low_refs[k][rows, :] = field.astype(BF16)
            return carry

        lax.fori_loop(0, size // LANES // mt, tile, 0)


def gather_heat(recv, base, gain, following, slope, spans):
    samples = base.shape[1]
    slots = recv.shape[0] * CAP
    count = sum(size for _, size in spans)
    shapes = [jax.ShapeDtypeStruct((size, samples), kind) for kind in (F32, BF16) for _, size in spans]
    return pl.pallas_call(
        functools.partial(gather_kernel, spans),
        out_shape=tuple(shapes),
        in_specs=[HBM] * 5,
        out_specs=(VMEM,) * len(shapes),
        scratch_shapes=[
            pltpu.VMEM(recv.shape, BF16),
            pltpu.VMEM((4, count, samples), F32),
            pltpu.VMEM((LANES, slots), BF16),
            pltpu.VMEM((16, slots), BF16),
            pltpu.VMEM((slots, 2 * samples), BF16),
            pltpu.SemaphoreType.DMA((PARTS,)),
            pltpu.SemaphoreType.DMA((4 * len(spans),)),
        ],
        compiler_params=params(52),
        cost_estimate=pl.CostEstimate(flops=4 * slots * count * samples, bytes_accessed=8_000_000, transcendentals=0),
        name="gather_heat",
    )(recv, base, gain, following, slope)


def turn_kernel(meta_ref, turned_ref):
    for g in range(meta_ref.shape[0] // 16):
        stacked = jnp.concatenate([meta_ref[g * 16 + j].astype(F32) for j in range(16)], axis=0)
        turned_ref[g] = stacked.T


def turn(meta):
    groups = meta.shape[0] // 16
    return pl.pallas_call(
        turn_kernel,
        out_shape=jax.ShapeDtypeStruct((groups, CAP, LANES), F32),
        in_specs=[VMEM],
        out_specs=VMEM,
        compiler_params=params(8),
        name="turn",
    )(meta)


def last_kernel(cols_ref, cond_ref, left_ref, head_ref, mid_ref, tail_ref, right_ref, next_head, next_mid, next_tail, gain_ref, turned_ref, temp_hbm, back_ref, window_ref, temp, pair, temp_sem):
    fill(window_ref, left_ref, head_ref, mid_ref, tail_ref, right_ref)
    blocks, size, _ = cond_ref.shape
    nodes, samples = gain_ref.shape
    groups = turned_ref.shape[0]
    tiles = nodes // LANES

    first = 0
    for ref in (next_head, next_mid, next_tail):

        def step(i, carry):
            r = first + i
            rows = pl.ds(pl.multiple_of(r * size, size), size)
            applied = apply_blocks(cols_ref, cond_ref, window_ref, r)
            field = ref[pl.ds(pl.multiple_of(i * size, size), size), :] - applied * gain_ref[rows, :]
            temp[rows, :] = field
            top = field.astype(BF16)
            rest = (field - top.astype(F32)).astype(BF16)
            pair[rows, :] = jnp.concatenate([top, rest], axis=1)
            return carry

        lax.fori_loop(0, ref.shape[0] // size, step, 0, unroll=8 if ref is next_mid else 12)
        first += ref.shape[0] // size
    temp_copy = pltpu.make_async_copy(temp, temp_hbm, temp_sem)
    temp_copy.start()
    lane = iota((CAP, LANES), 1).astype(F32)

    def send(g, carry):
        for j in range(16):
            own = turned_ref[g, :, j * META : j * META + 4]
            low = jnp.broadcast_to(own[:, 3:4], (CAP, LANES))
            low_hit = jnp.where(low == lane, 1.0, 0.0).astype(BF16)
            high = jnp.broadcast_to(own[:, 2:3], (CAP, LANES))
            hits = [low_hit * jnp.where(high == float(t), 1.0, 0.0).astype(BF16) for t in range(tiles)]
            both = dot(jnp.concatenate(hits, axis=1), pair[...])
            seen = both[:, :samples] + both[:, samples:]
            back_ref[g * 16 + j] = (own[:, 0:1] * (1.0 + own[:, 1:2] * seen)).astype(BF16)
        return carry

    lax.fori_loop(0, groups, send, 0)
    temp_copy.wait()


def last_sweep(cols, cond, window, following, gain, turned):
    nodes, samples = gain.shape
    peers = turned.shape[0] * 16
    return pl.pallas_call(
        last_kernel,
        out_shape=(
            jax.ShapeDtypeStruct((nodes, samples), F32),
            jax.ShapeDtypeStruct((peers, CAP, samples), BF16),
        ),
        in_specs=[SMEM] + [VMEM] * 11,
        out_specs=(HBM, VMEM),
        scratch_shapes=[
            pltpu.VMEM((sum(part.shape[0] for part in window), samples), BF16),
            pltpu.VMEM((nodes, samples), F32),
            pltpu.VMEM((nodes, 2 * samples), BF16),
            pltpu.SemaphoreType.DMA,
        ],
        compiler_params=params(24),
        name="last_sweep",
    )(cols, cond, *window, *following, gain, turned)


def unpack_kernel(slot_ref, back_ref, out_hbm, wide, picked, out, sems):
    peers, _, samples = back_ref.shape
    for p in range(peers):
        wide[p * CAP : (p + 1) * CAP] = back_ref[p].astype(F32)
    chunks = slot_ref.shape[0] // PARTS

    def gather(r, carry):
        for lane in range(LANES):
            picked[pl.ds(r * LANES + lane, 1), :] = wide[pl.ds(slot_ref[r, lane], 1), :]
        return carry

    copies = []
    for g in range(PARTS):
        lax.fori_loop(g * chunks, (g + 1) * chunks, gather, 0)
        span = pl.ds(g * chunks * LANES, chunks * LANES)
        out[span, :] = picked[span, :].astype(BF16)
        copies.append(pltpu.make_async_copy(out.at[span], out_hbm.at[span], sems.at[g]))
        copies[g].start()
    for copy in copies:
        copy.wait()


def unpack(slots, back):
    peers, _, samples = back.shape
    count = slots.shape[0] * slots.shape[1]
    return pl.pallas_call(
        unpack_kernel,
        out_shape=jax.ShapeDtypeStruct((count, samples), BF16),
        in_specs=[SMEM, VMEM],
        out_specs=HBM,
        scratch_shapes=[
            pltpu.VMEM((peers * CAP, samples), F32),
            pltpu.VMEM((count, samples), F32),
            pltpu.VMEM((count, samples), BF16),
            pltpu.SemaphoreType.DMA((PARTS,)),
        ],
        compiler_params=params(24),
        name="unpack",
    )(slots, back)


def halo(head, tail):
    axes = ("dom", "blk")
    count = lax.axis_size(axes)
    left = lax.ppermute(tail, axes, [(i, (i + 1) % count) for i in range(count)])
    right = lax.ppermute(head, axes, [((i + 1) % count, i) for i in range(count)])
    return left, right


def body(current, resistivity, temp_coef, dest_part, dest_row, temp_old, heat_cap, conduction, block_cols):
    count, samples = current.shape
    peers = lax.axis_size("dom")
    blocks, size, _ = conduction.shape
    chunks = count // LANES
    width = HB * size
    left, right = halo(temp_old[:width], temp_old[-width:])
    send, slots = pack(
        dest_part.reshape(chunks, LANES),
        dest_row.reshape(chunks, LANES),
        resistivity.reshape(chunks, LANES),
        temp_coef.reshape(chunks, LANES),
        current,
        peers,
    )
    send, _, _ = lax.optimization_barrier((send, left, right))
    recv = lax.all_to_all(send, "dom", split_axis=0, concat_axis=0, tiled=True)
    devices = lax.axis_size(("dom", "blk"))
    first_block = lax.axis_index(("dom", "blk")) * blocks
    cols = jnp.mod(block_cols - first_block + HB, blocks * devices)
    base, gain, following, slope = first_sweep(cols, conduction, left, temp_old, right, heat_cap[:, None])
    nodes = temp_old.shape[0]
    outer = ((0, width), (nodes - width, width))
    inner = ((width, nodes - 2 * width),)
    next_head, next_tail, head, tail = gather_heat(recv, base, gain, following, slope, outer)
    left, right = halo(head, tail)
    next_mid, mid = gather_heat(recv, base, gain, following, slope, inner)
    window = (left, head, mid, tail, right)
    temp, back = last_sweep(cols, conduction, window, (next_head, next_mid, next_tail), gain, turn(recv[:, CAP:]))
    returned = lax.all_to_all(back, "dom", split_axis=0, concat_axis=0, tiled=True)
    return temp, unpack(slots, returned)


def solution(mesh):
    both = ("dom", "blk")
    placed = (
        P(both, None),
        P(both),
        P(both),
        P(both, None),
        P(both),
        P(both, None),
        P(both),
        P(both, None, None),
        P(both, None),
    )
    return jax.shard_map(
        body,
        mesh=mesh,
        in_specs=placed,
        out_specs=(P(both, None), P(both, None)),
        check_vma=False,
    )
```

```python
import functools

import jax
import jax.numpy as jnp
from jax import lax
from jax.experimental import pallas as pl
from jax.experimental.pallas import tpu as pltpu
from jax.sharding import PartitionSpec as P

HB = 12
CAP = 128
META = 8
PARTS = 4
LANES = 128
F32 = jnp.float32
BF16 = jnp.bfloat16
VMEM = pl.BlockSpec(memory_space=pltpu.VMEM)
SMEM = pl.BlockSpec(memory_space=pltpu.SMEM)
HBM = pl.BlockSpec(memory_space=pltpu.HBM)


def params(mib):
    return pltpu.CompilerParams(vmem_limit_bytes=mib * 1024 * 1024)


def dot(a, b):
    return jnp.dot(a, b, preferred_element_type=F32)


def iota(shape, dim):
    return lax.broadcasted_iota(jnp.int32, shape, dim)


def pack_kernel(part_ref, row_ref, res_ref, coef_ref, cur_hbm, send_ref, slot_ref, slot_vmem, cur, wide, spread, ready, sem, out_sems):
    peers = send_ref.shape[0]
    fetch = pltpu.make_async_copy(cur_hbm, cur, sem.at[0])
    fetch.start()
    chunks = part_ref.shape[0]
    before = (iota((LANES, LANES), 0) < iota((LANES, LANES), 1)).astype(BF16)
    counter = jnp.concatenate([before, jnp.ones((LANES, LANES), BF16)], axis=1)
    carry = jnp.zeros((peers, LANES), F32)
    meta = jnp.zeros((4 * peers, LANES), F32)
    part = part_ref[...]
    row = row_ref[...]
    high = lax.shift_right_logical(row, 7).astype(F32)
    low = jnp.bitwise_and(row, 127).astype(F32)
    res = res_ref[...].astype(F32)
    coef = coef_ref[...].astype(F32)
    slots = []
    for r in range(chunks):
        hit = (iota((peers, LANES), 0) == part[r : r + 1]).astype(F32)
        counted = dot(hit.astype(BF16), counter)
        rank = jnp.sum(hit * (counted[:, :LANES] + carry), axis=0, keepdims=True)
        carry = carry + counted[:, LANES:]
        rank = rank.astype(jnp.int32)
        slots.append(part[r : r + 1] * CAP + rank)
        place = (iota((CAP, LANES), 0) == rank).astype(F32).astype(BF16)
        values = jnp.concatenate(
            [hit * res[r : r + 1], hit * coef[r : r + 1], hit * high[r : r + 1], hit * low[r : r + 1]], axis=0
        ).astype(BF16)
        meta = meta + lax.dot_general(values, place, (((1,), (1,)), ((), ())), preferred_element_type=F32)
    slot_vmem[...] = jnp.concatenate(slots, axis=0)
    copy = pltpu.make_async_copy(slot_vmem, slot_ref, sem.at[1])
    copy.start()
    spread[...] = jnp.zeros(spread.shape, F32)
    fetch.wait()
    wide[...] = cur[...].astype(F32)
    copy.wait()

    def scatter(r, carry):
        for lane in range(LANES):
            spread[pl.ds(slot_ref[r, lane], 1), :] = wide[pl.ds(r * LANES + lane, 1), :]
        return carry

    lax.fori_loop(0, chunks, scatter, 0)
    rows = [meta[i * peers : (i + 1) * peers] for i in range(4)]
    group = peers // PARTS
    copies = []
    for g in range(PARTS):
        for p in range(g * group, (g + 1) * group):
            own = jnp.concatenate([m[p : p + 1] for m in rows] + [jnp.zeros((META - 4, LANES), F32)], axis=0)
            ready[p, :CAP] = spread[p * CAP : (p + 1) * CAP].astype(BF16)
            ready[p, CAP:] = own.astype(BF16)
        span = pl.ds(g * group, group)
        copies.append(pltpu.make_async_copy(ready.at[span], send_ref.at[span], out_sems.at[g]))
        copies[g].start()
    for copy in copies:
        copy.wait()


def pack(part, row, res, coef, cur, peers):
    count, samples = cur.shape
    chunks = count // LANES
    return pl.pallas_call(
        pack_kernel,
        out_shape=(
            jax.ShapeDtypeStruct((peers, CAP + META, samples), BF16),
            jax.ShapeDtypeStruct((chunks, LANES), jnp.int32),
        ),
        in_specs=[VMEM] * 4 + [HBM],
        out_specs=(HBM, SMEM),
        scratch_shapes=[
            pltpu.VMEM((chunks, LANES), jnp.int32),
            pltpu.VMEM((count, samples), BF16),
            pltpu.VMEM((count, samples), F32),
            pltpu.VMEM((peers * CAP, samples), F32),
            pltpu.VMEM((peers, CAP + META, samples), BF16),
            pltpu.SemaphoreType.DMA((2,)),
            pltpu.SemaphoreType.DMA((PARTS,)),
        ],
        compiler_params=params(60),
        cost_estimate=pl.CostEstimate(flops=8_000_000_000, bytes_accessed=4_000_000, transcendentals=0),
        name="pack",
    )(part, row, res, coef, cur)


def apply_blocks(cols_ref, cond_ref, window_ref, r):
    size = cond_ref.shape[1]
    picked = []
    for k in range(cols_ref.shape[1]):
        start = pl.multiple_of(cols_ref[r, k] * size, size)
        picked.append(window_ref[pl.ds(start, size), :])
    return dot(cond_ref[r], jnp.concatenate(picked, axis=0))


def fill(window_ref, *parts):
    start = 0
    for ref in parts:
        window_ref[start : start + ref.shape[0]] = ref[...].astype(BF16)
        start += ref.shape[0]


def first_kernel(cols_ref, cond_ref, left_ref, old_ref, right_ref, cap_ref, base_ref, gain_ref, next_ref, slope_ref, window_ref):
    fill(window_ref, left_ref, old_ref, right_ref)
    blocks, size, _ = cond_ref.shape
    samples = window_ref.shape[1]
    eye = iota((size, size), 0) == iota((size, size), 1)

    def step(r, carry):
        rows = pl.ds(pl.multiple_of(r * size, size), size)
        applied = apply_blocks(cols_ref, cond_ref, window_ref, r)
        corner = cond_ref[r, :, :size].astype(F32)
        diag = jnp.sum(jnp.where(eye, corner, 0.0), axis=1, keepdims=True)
        cap = cap_ref[rows, :]
        gain = jnp.broadcast_to(1.0 / (diag + cap), (size, samples))
        cap = jnp.broadcast_to(cap, (size, samples))
        old = old_ref[rows, :]
        base = old - applied * gain
        share = cap * gain
        base_ref[rows, :] = base
        gain_ref[rows, :] = gain
        next_ref[rows, :] = base * (1.0 - share) + share * old
        slope_ref[rows, :] = gain * (2.0 - share)
        return carry

    lax.fori_loop(0, blocks, step, 0, unroll=8)


def first_sweep(cols, cond, left, old, right, cap):
    nodes, samples = old.shape
    return pl.pallas_call(
        first_kernel,
        out_shape=(jax.ShapeDtypeStruct((nodes, samples), F32),) * 4,
        in_specs=[SMEM] + [VMEM] * 5,
        out_specs=(VMEM,) * 4,
        scratch_shapes=[pltpu.VMEM((nodes + 2 * left.shape[0], samples), BF16)],
        compiler_params=params(48),
        cost_estimate=pl.CostEstimate(flops=8_000_000_000, bytes_accessed=8_000_000, transcendentals=0),
        name="first_sweep",
    )(cols, cond, left, old, right, cap)


STEP = 8


def gather_kernel(spans, turning, recv_hbm, base_hbm, gain_hbm, next_hbm, slope_hbm, *rest):
    count = len(spans)
    next_refs, low_refs = rest[:count], rest[count : 2 * count]
    turned_refs = rest[2 * count : 2 * count + turning]
    recv_ref, node_in, chosen, high, values, recv_sems, sems = rest[2 * count + turning :]
    peers = recv_ref.shape[0]
    group = peers // PARTS
    samples = node_in.shape[2]
    arrivals = []
    for g in range(PARTS):
        span = pl.ds(g * group, group)
        arrivals.append(pltpu.make_async_copy(recv_hbm.at[span], recv_ref.at[span], recv_sems.at[g]))
        arrivals[g].start()
    copies, offsets, offset = [], [], 0
    for k, (first, size) in enumerate(spans):
        for i, ref in enumerate((base_hbm, gain_hbm, next_hbm, slope_hbm)):
            target = node_in.at[i, pl.ds(offset, size)]
            copies.append(pltpu.make_async_copy(ref.at[pl.ds(first, size)], target, sems.at[4 * k + i]))
        offsets.append(offset)
        offset += size
    for copy in copies:
        copy.start()
    sub = iota((LANES, LANES), 0).astype(F32)

    def split(p, carry):
        rows = pl.ds(pl.multiple_of(p * CAP, CAP), CAP)
        cur = recv_ref[p, :CAP].astype(F32)
        square = cur * cur
        top = square.astype(BF16)
        rest = (square - top.astype(F32)).astype(BF16)
        values[rows, :] = jnp.concatenate([top, rest], axis=1)
        meta = recv_ref[p, CAP:].astype(F32)
        chosen[:, rows] = jnp.where(sub == meta[3:4], meta[0:1], 0.0).astype(BF16)
        high[:, rows] = jnp.broadcast_to(meta[2:3], (16, CAP)).astype(BF16)
        return carry

    for g in range(PARTS):
        arrivals[g].wait()
        lax.fori_loop(g * group, (g + 1) * group, split, 0, unroll=4)
    for ref in turned_refs:
        for g in range(peers // 16):
            stacked = jnp.concatenate([recv_ref[g * 16 + j, CAP:].astype(F32) for j in range(16)], axis=0)
            ref[g] = stacked.T
    part = peers * CAP // STEP
    for copy in copies:
        copy.wait()
    for k, (first, size) in enumerate(spans):
        mt = next(m for m in (6, 4, 3, 2, 1) if size // LANES % m == 0)

        def tile(t, carry):
            both = jnp.zeros((mt * LANES, 2 * samples), F32)
            for c in range(STEP):
                cols = slice(c * part, (c + 1) * part)
                own_base = chosen[:, cols]
                own_high = high[:, cols]
                hits = []
                for i in range(mt):
                    own = (first // LANES + t * mt + i).astype(F32).astype(BF16)
                    hit = (own_high == own).astype(BF16)
                    hits.append(own_base * jnp.concatenate([hit] * (LANES // 16), axis=0))
                both = both + dot(jnp.concatenate(hits, axis=0), values[cols, :])
            start = pl.multiple_of(t * mt * LANES, LANES)
            rows = pl.ds(start, mt * LANES)
            here = pl.ds(offsets[k] + start, mt * LANES)
            heat = both[:, :samples] + both[:, samples:]
            field = node_in[0, here, :] + heat * node_in[1, here, :]
            next_refs[k][rows, :] = node_in[2, here, :] + heat * node_in[3, here, :]
            low_refs[k][rows, :] = field.astype(BF16)
            return carry

        lax.fori_loop(0, size // LANES // mt, tile, 0)


def gather_heat(recv, base, gain, following, slope, spans, turning=0):
    samples = base.shape[1]
    slots = recv.shape[0] * CAP
    count = sum(size for _, size in spans)
    shapes = [jax.ShapeDtypeStruct((size, samples), kind) for kind in (F32, BF16) for _, size in spans]
    shapes += [jax.ShapeDtypeStruct((recv.shape[0] // 16, CAP, LANES), F32)] * turning
    return pl.pallas_call(
        functools.partial(gather_kernel, spans, turning),
        out_shape=tuple(shapes),
        in_specs=[HBM] * 5,
        out_specs=(VMEM,) * len(shapes),
        scratch_shapes=[
            pltpu.VMEM(recv.shape, BF16),
            pltpu.VMEM((4, count, samples), F32),
            pltpu.VMEM((LANES, slots), BF16),
            pltpu.VMEM((16, slots), BF16),
            pltpu.VMEM((slots, 2 * samples), BF16),
            pltpu.SemaphoreType.DMA((PARTS,)),
            pltpu.SemaphoreType.DMA((4 * len(spans),)),
        ],
        compiler_params=params(52),
        cost_estimate=pl.CostEstimate(flops=4 * slots * count * samples, bytes_accessed=8_000_000, transcendentals=0),
        name="gather_heat",
    )(recv, base, gain, following, slope)


def last_kernel(cols_ref, cond_ref, left_ref, head_ref, mid_ref, tail_ref, right_ref, next_head, next_mid, next_tail, gain_ref, turned_ref, temp_hbm, back_ref, window_ref, temp, pair, temp_sem):
    fill(window_ref, left_ref, head_ref, mid_ref, tail_ref, right_ref)
    blocks, size, _ = cond_ref.shape
    nodes, samples = gain_ref.shape
    groups = turned_ref.shape[0]
    tiles = nodes // LANES

    first = 0
    for ref in (next_head, next_mid, next_tail):

        def step(i, carry):
            r = first + i
            rows = pl.ds(pl.multiple_of(r * size, size), size)
            applied = apply_blocks(cols_ref, cond_ref, window_ref, r)
            field = ref[pl.ds(pl.multiple_of(i * size, size), size), :] - applied * gain_ref[rows, :]
            temp[rows, :] = field
            top = field.astype(BF16)
            rest = (field - top.astype(F32)).astype(BF16)
            pair[rows, :] = jnp.concatenate([top, rest], axis=1)
            return carry

        lax.fori_loop(0, ref.shape[0] // size, step, 0, unroll=8 if ref is next_mid else 12)
        first += ref.shape[0] // size
    temp_copy = pltpu.make_async_copy(temp, temp_hbm, temp_sem)
    temp_copy.start()
    lane = iota((CAP, LANES), 1).astype(F32)

    def send(g, carry):
        for j in range(16):
            own = turned_ref[g, :, j * META : j * META + 4]
            low = jnp.broadcast_to(own[:, 3:4], (CAP, LANES))
            low_hit = jnp.where(low == lane, 1.0, 0.0).astype(BF16)
            high = jnp.broadcast_to(own[:, 2:3], (CAP, LANES))
            hits = [low_hit * jnp.where(high == float(t), 1.0, 0.0).astype(BF16) for t in range(tiles)]
            both = dot(jnp.concatenate(hits, axis=1), pair[...])
            seen = both[:, :samples] + both[:, samples:]
            back_ref[g * 16 + j] = (own[:, 0:1] * (1.0 + own[:, 1:2] * seen)).astype(BF16)
        return carry

    lax.fori_loop(0, groups, send, 0)
    temp_copy.wait()


def last_sweep(cols, cond, window, following, gain, turned):
    nodes, samples = gain.shape
    peers = turned.shape[0] * 16
    return pl.pallas_call(
        last_kernel,
        out_shape=(
            jax.ShapeDtypeStruct((nodes, samples), F32),
            jax.ShapeDtypeStruct((peers, CAP, samples), BF16),
        ),
        in_specs=[SMEM] + [VMEM] * 11,
        out_specs=(HBM, VMEM),
        scratch_shapes=[
            pltpu.VMEM((sum(part.shape[0] for part in window), samples), BF16),
            pltpu.VMEM((nodes, samples), F32),
            pltpu.VMEM((nodes, 2 * samples), BF16),
            pltpu.SemaphoreType.DMA,
        ],
        compiler_params=params(24),
        name="last_sweep",
    )(cols, cond, *window, *following, gain, turned)


def unpack_kernel(slot_ref, back_ref, out_hbm, wide, picked, out, sems):
    peers, _, samples = back_ref.shape
    for p in range(peers):
        wide[p * CAP : (p + 1) * CAP] = back_ref[p].astype(F32)
    chunks = slot_ref.shape[0] // PARTS

    def gather(r, carry):
        for lane in range(LANES):
            picked[pl.ds(r * LANES + lane, 1), :] = wide[pl.ds(slot_ref[r, lane], 1), :]
        return carry

    copies = []
    for g in range(PARTS):
        lax.fori_loop(g * chunks, (g + 1) * chunks, gather, 0)
        span = pl.ds(g * chunks * LANES, chunks * LANES)
        out[span, :] = picked[span, :].astype(BF16)
        copies.append(pltpu.make_async_copy(out.at[span], out_hbm.at[span], sems.at[g]))
        copies[g].start()
    for copy in copies:
        copy.wait()


def unpack(slots, back):
    peers, _, samples = back.shape
    count = slots.shape[0] * slots.shape[1]
    return pl.pallas_call(
        unpack_kernel,
        out_shape=jax.ShapeDtypeStruct((count, samples), BF16),
        in_specs=[SMEM, VMEM],
        out_specs=HBM,
        scratch_shapes=[
            pltpu.VMEM((peers * CAP, samples), F32),
            pltpu.VMEM((count, samples), F32),
            pltpu.VMEM((count, samples), BF16),
            pltpu.SemaphoreType.DMA((PARTS,)),
        ],
        compiler_params=params(24),
        name="unpack",
    )(slots, back)


def halo(head, tail):
    axes = ("dom", "blk")
    count = lax.axis_size(axes)
    left = lax.ppermute(tail, axes, [(i, (i + 1) % count) for i in range(count)])
    right = lax.ppermute(head, axes, [((i + 1) % count, i) for i in range(count)])
    return left, right


def body(current, resistivity, temp_coef, dest_part, dest_row, temp_old, heat_cap, conduction, block_cols):
    count, samples = current.shape
    peers = lax.axis_size("dom")
    blocks, size, _ = conduction.shape
    chunks = count // LANES
    width = HB * size
    left, right = halo(temp_old[:width], temp_old[-width:])
    send, slots = pack(
        dest_part.reshape(chunks, LANES),
        dest_row.reshape(chunks, LANES),
        resistivity.reshape(chunks, LANES),
        temp_coef.reshape(chunks, LANES),
        current,
        peers,
    )
    send, _, _ = lax.optimization_barrier((send, left, right))
    recv = lax.all_to_all(send, "dom", split_axis=0, concat_axis=0, tiled=True)
    devices = lax.axis_size(("dom", "blk"))
    first_block = lax.axis_index(("dom", "blk")) * blocks
    cols = jnp.mod(block_cols - first_block + HB, blocks * devices)
    base, gain, following, slope = first_sweep(cols, conduction, left, temp_old, right, heat_cap[:, None])
    nodes = temp_old.shape[0]
    outer = ((0, width), (nodes - width, width))
    inner = ((width, nodes - 2 * width),)
    next_head, next_tail, head, tail = gather_heat(recv, base, gain, following, slope, outer)
    left, right = halo(head, tail)
    next_mid, mid, turned = gather_heat(recv, base, gain, following, slope, inner, 1)
    window = (left, head, mid, tail, right)
    temp, back = last_sweep(cols, conduction, window, (next_head, next_mid, next_tail), gain, turned)
    returned = lax.all_to_all(back, "dom", split_axis=0, concat_axis=0, tiled=True)
    return temp, unpack(slots, returned)


def solution(mesh):
    both = ("dom", "blk")
    placed = (
        P(both, None),
        P(both),
        P(both),
        P(both, None),
        P(both),
        P(both, None),
        P(both),
        P(both, None, None),
        P(both, None),
    )
    return jax.shard_map(
        body,
        mesh=mesh,
        in_specs=placed,
        out_specs=(P(both, None), P(both, None)),
        check_vma=False,
    )
```

```python
import functools

import jax
import jax.numpy as jnp
from jax import lax
from jax.experimental import pallas as pl
from jax.experimental.pallas import tpu as pltpu
from jax.sharding import PartitionSpec as P

HB = 12
CAP = 128
META = 8
PARTS = 4
LANES = 128
F32 = jnp.float32
BF16 = jnp.bfloat16
VMEM = pl.BlockSpec(memory_space=pltpu.VMEM)
SMEM = pl.BlockSpec(memory_space=pltpu.SMEM)
HBM = pl.BlockSpec(memory_space=pltpu.HBM)


def params(mib):
    return pltpu.CompilerParams(vmem_limit_bytes=mib * 1024 * 1024)


def dot(a, b):
    return jnp.dot(a, b, preferred_element_type=F32)


def iota(shape, dim):
    return lax.broadcasted_iota(jnp.int32, shape, dim)


def pack_kernel(part_ref, row_ref, res_ref, coef_ref, cur_hbm, send_ref, slot_ref, slot_vmem, cur, wide, spread, ready, sem, out_sems):
    peers = send_ref.shape[0]
    fetch = pltpu.make_async_copy(cur_hbm, cur, sem.at[0])
    fetch.start()
    chunks = part_ref.shape[0]
    before = (iota((LANES, LANES), 0) < iota((LANES, LANES), 1)).astype(BF16)
    counter = jnp.concatenate([before, jnp.ones((LANES, LANES), BF16)], axis=1)
    carry = jnp.zeros((peers, LANES), F32)
    meta = jnp.zeros((4 * peers, LANES), F32)
    part = part_ref[...]
    row = row_ref[...]
    high = lax.shift_right_logical(row, 7).astype(F32)
    low = jnp.bitwise_and(row, 127).astype(F32)
    res = res_ref[...].astype(F32)
    coef = coef_ref[...].astype(F32)
    slots = []
    for r in range(chunks):
        hit = (iota((peers, LANES), 0) == part[r : r + 1]).astype(F32)
        counted = dot(hit.astype(BF16), counter)
        rank = jnp.sum(hit * (counted[:, :LANES] + carry), axis=0, keepdims=True)
        carry = carry + counted[:, LANES:]
        rank = rank.astype(jnp.int32)
        slots.append(part[r : r + 1] * CAP + rank)
        place = (iota((CAP, LANES), 0) == rank).astype(F32).astype(BF16)
        values = jnp.concatenate(
            [hit * res[r : r + 1], hit * coef[r : r + 1], hit * high[r : r + 1], hit * low[r : r + 1]], axis=0
        ).astype(BF16)
        meta = meta + lax.dot_general(values, place, (((1,), (1,)), ((), ())), preferred_element_type=F32)
    slot_vmem[...] = jnp.concatenate(slots, axis=0)
    copy = pltpu.make_async_copy(slot_vmem, slot_ref, sem.at[1])
    copy.start()
    spread[...] = jnp.zeros(spread.shape, F32)
    fetch.wait()
    wide[...] = cur[...].astype(F32)
    copy.wait()

    def scatter(r, carry):
        for lane in range(LANES):
            spread[pl.ds(slot_ref[r, lane], 1), :] = wide[pl.ds(r * LANES + lane, 1), :]
        return carry

    lax.fori_loop(0, chunks, scatter, 0)
    rows = [meta[i * peers : (i + 1) * peers] for i in range(4)]
    group = peers // PARTS
    copies = []
    for g in range(PARTS):
        for p in range(g * group, (g + 1) * group):
            own = jnp.concatenate([m[p : p + 1] for m in rows] + [jnp.zeros((META - 4, LANES), F32)], axis=0)
            ready[p, :CAP] = spread[p * CAP : (p + 1) * CAP].astype(BF16)
            ready[p, CAP:] = own.astype(BF16)
        span = pl.ds(g * group, group)
        copies.append(pltpu.make_async_copy(ready.at[span], send_ref.at[span], out_sems.at[g]))
        copies[g].start()
    for copy in copies:
        copy.wait()


def pack(part, row, res, coef, cur, peers):
    count, samples = cur.shape
    chunks = count // LANES
    return pl.pallas_call(
        pack_kernel,
        out_shape=(
            jax.ShapeDtypeStruct((peers, CAP + META, samples), BF16),
            jax.ShapeDtypeStruct((chunks, LANES), jnp.int32),
        ),
        in_specs=[VMEM] * 4 + [HBM],
        out_specs=(HBM, SMEM),
        scratch_shapes=[
            pltpu.VMEM((chunks, LANES), jnp.int32),
            pltpu.VMEM((count, samples), BF16),
            pltpu.VMEM((count, samples), F32),
            pltpu.VMEM((peers * CAP, samples), F32),
            pltpu.VMEM((peers, CAP + META, samples), BF16),
            pltpu.SemaphoreType.DMA((2,)),
            pltpu.SemaphoreType.DMA((PARTS,)),
        ],
        compiler_params=params(60),
        cost_estimate=pl.CostEstimate(flops=8_000_000_000, bytes_accessed=4_000_000, transcendentals=0),
        name="pack",
    )(part, row, res, coef, cur)


def apply_blocks(cols_ref, cond_ref, window_ref, r):
    size = cond_ref.shape[1]
    picked = []
    for k in range(cols_ref.shape[1]):
        start = pl.multiple_of(cols_ref[r, k] * size, size)
        picked.append(window_ref[pl.ds(start, size), :])
    return dot(cond_ref[r], jnp.concatenate(picked, axis=0))


def fill(window_ref, *parts):
    start = 0
    for ref in parts:
        window_ref[start : start + ref.shape[0]] = ref[...].astype(BF16)
        start += ref.shape[0]


def first_kernel(cols_ref, cond_ref, left_ref, old_ref, right_ref, cap_ref, base_ref, gain_ref, next_ref, slope_ref, window_ref):
    fill(window_ref, left_ref, old_ref, right_ref)
    blocks, size, _ = cond_ref.shape
    samples = window_ref.shape[1]
    eye = iota((size, size), 0) == iota((size, size), 1)

    def step(r, carry):
        rows = pl.ds(pl.multiple_of(r * size, size), size)
        applied = apply_blocks(cols_ref, cond_ref, window_ref, r)
        corner = cond_ref[r, :, :size].astype(F32)
        diag = jnp.sum(jnp.where(eye, corner, 0.0), axis=1, keepdims=True)
        cap = cap_ref[rows, :]
        gain = jnp.broadcast_to(1.0 / (diag + cap), (size, samples))
        cap = jnp.broadcast_to(cap, (size, samples))
        old = old_ref[rows, :]
        base = old - applied * gain
        share = cap * gain
        base_ref[rows, :] = base
        gain_ref[rows, :] = gain
        next_ref[rows, :] = base * (1.0 - share) + share * old
        slope_ref[rows, :] = gain * (2.0 - share)
        return carry

    lax.fori_loop(0, blocks, step, 0, unroll=8)


def first_sweep(cols, cond, left, old, right, cap):
    nodes, samples = old.shape
    return pl.pallas_call(
        first_kernel,
        out_shape=(jax.ShapeDtypeStruct((nodes, samples), F32),) * 4,
        in_specs=[SMEM] + [VMEM] * 5,
        out_specs=(VMEM,) * 4,
        scratch_shapes=[pltpu.VMEM((nodes + 2 * left.shape[0], samples), BF16)],
        compiler_params=params(48),
        cost_estimate=pl.CostEstimate(flops=8_000_000_000, bytes_accessed=8_000_000, transcendentals=0),
        name="first_sweep",
    )(cols, cond, left, old, right, cap)


STEP = 8


def gather_kernel(spans, turning, recv_hbm, base_hbm, gain_hbm, next_hbm, slope_hbm, *rest):
    count = len(spans)
    next_refs, low_refs = rest[:count], rest[count : 2 * count]
    turned_refs = rest[2 * count : 2 * count + turning]
    recv_ref, node_in, chosen, high, values, recv_sems, sems = rest[2 * count + turning :]
    peers = recv_ref.shape[0]
    group = peers // PARTS
    samples = node_in.shape[2]
    arrivals = []
    for g in range(PARTS):
        span = pl.ds(g * group, group)
        arrivals.append(pltpu.make_async_copy(recv_hbm.at[span], recv_ref.at[span], recv_sems.at[g]))
        arrivals[g].start()
    copies, offsets, offset = [], [], 0
    for k, (first, size) in enumerate(spans):
        for i, ref in enumerate((base_hbm, gain_hbm, next_hbm, slope_hbm)):
            target = node_in.at[i, pl.ds(offset, size)]
            copies.append(pltpu.make_async_copy(ref.at[pl.ds(first, size)], target, sems.at[4 * k + i]))
        offsets.append(offset)
        offset += size
    for copy in copies:
        copy.start()
    sub = iota((LANES, LANES), 0).astype(F32)

    def split(p, carry):
        rows = pl.ds(pl.multiple_of(p * CAP, CAP), CAP)
        cur = recv_ref[p, :CAP].astype(F32)
        square = cur * cur
        top = square.astype(BF16)
        rest = (square - top.astype(F32)).astype(BF16)
        values[rows, :] = jnp.concatenate([top, rest], axis=1)
        meta = recv_ref[p, CAP:].astype(F32)
        chosen[:, rows] = jnp.where(sub == meta[3:4], meta[0:1], 0.0).astype(BF16)
        high[:, rows] = jnp.broadcast_to(meta[2:3], (16, CAP)).astype(BF16)
        return carry

    for g in range(PARTS):
        arrivals[g].wait()
        lax.fori_loop(g * group, (g + 1) * group, split, 0, unroll=4)
    for ref in turned_refs:
        for g in range(peers // 16):
            stacked = jnp.concatenate([recv_ref[g * 16 + j, CAP:].astype(F32) for j in range(16)], axis=0)
            ref[g] = stacked.T
    part = peers * CAP // STEP
    for copy in copies:
        copy.wait()
    for k, (first, size) in enumerate(spans):
        mt = next(m for m in (6, 4, 3, 2, 1) if size // LANES % m == 0)

        def tile(t, carry):
            both = jnp.zeros((mt * LANES, 2 * samples), F32)
            for c in range(STEP):
                cols = slice(c * part, (c + 1) * part)
                own_base = chosen[:, cols]
                own_high = high[:, cols]
                hits = []
                for i in range(mt):
                    own = (first // LANES + t * mt + i).astype(F32).astype(BF16)
                    hit = (own_high == own).astype(BF16)
                    hits.append(own_base * jnp.concatenate([hit] * (LANES // 16), axis=0))
                both = both + dot(jnp.concatenate(hits, axis=0), values[cols, :])
            start = pl.multiple_of(t * mt * LANES, LANES)
            rows = pl.ds(start, mt * LANES)
            here = pl.ds(offsets[k] + start, mt * LANES)
            heat = both[:, :samples] + both[:, samples:]
            field = node_in[0, here, :] + heat * node_in[1, here, :]
            next_refs[k][rows, :] = node_in[2, here, :] + heat * node_in[3, here, :]
            low_refs[k][rows, :] = field.astype(BF16)
            return carry

        lax.fori_loop(0, size // LANES // mt, tile, 0)


def gather_heat(recv, base, gain, following, slope, spans, turning=0):
    samples = base.shape[1]
    slots = recv.shape[0] * CAP
    count = sum(size for _, size in spans)
    shapes = [jax.ShapeDtypeStruct((size, samples), kind) for kind in (F32, BF16) for _, size in spans]
    shapes += [jax.ShapeDtypeStruct((recv.shape[0] // 16, CAP, LANES), F32)] * turning
    return pl.pallas_call(
        functools.partial(gather_kernel, spans, turning),
        out_shape=tuple(shapes),
        in_specs=[HBM] * 5,
        out_specs=(VMEM,) * len(shapes),
        scratch_shapes=[
            pltpu.VMEM(recv.shape, BF16),
            pltpu.VMEM((4, count, samples), F32),
            pltpu.VMEM((LANES, slots), BF16),
            pltpu.VMEM((16, slots), BF16),
            pltpu.VMEM((slots, 2 * samples), BF16),
            pltpu.SemaphoreType.DMA((PARTS,)),
            pltpu.SemaphoreType.DMA((4 * len(spans),)),
        ],
        compiler_params=params(52),
        cost_estimate=pl.CostEstimate(flops=4 * slots * count * samples, bytes_accessed=8_000_000, transcendentals=0),
        name="gather_heat",
    )(recv, base, gain, following, slope)


def last_kernel(cols_ref, cond_ref, left_ref, head_ref, mid_ref, tail_ref, right_ref, next_head, next_mid, next_tail, gain_ref, turned_ref, temp_hbm, back_ref, window_ref, temp, pair, temp_sem):
    fill(window_ref, left_ref, head_ref, mid_ref, tail_ref, right_ref)
    blocks, size, _ = cond_ref.shape
    nodes, samples = gain_ref.shape
    groups = turned_ref.shape[0]
    tiles = nodes // LANES

    first = 0
    for ref in (next_head, next_mid, next_tail):

        def step(i, carry):
            r = first + i
            rows = pl.ds(pl.multiple_of(r * size, size), size)
            applied = apply_blocks(cols_ref, cond_ref, window_ref, r)
            field = ref[pl.ds(pl.multiple_of(i * size, size), size), :] - applied * gain_ref[rows, :]
            temp[rows, :] = field
            top = field.astype(BF16)
            rest = (field - top.astype(F32)).astype(BF16)
            pair[rows, :] = jnp.concatenate([top, rest], axis=1)
            return carry

        lax.fori_loop(0, ref.shape[0] // size, step, 0, unroll=8 if ref is next_mid else 12)
        first += ref.shape[0] // size
    temp_copy = pltpu.make_async_copy(temp, temp_hbm, temp_sem)
    temp_copy.start()
    lane = iota((CAP, LANES), 1).astype(F32)

    def send(g, carry):
        for j in range(16):
            own = turned_ref[g, :, j * META : j * META + 4]
            low = jnp.broadcast_to(own[:, 3:4], (CAP, LANES))
            low_hit = jnp.where(low == lane, 1.0, 0.0).astype(BF16)
            high = jnp.broadcast_to(own[:, 2:3], (CAP, LANES))
            hits = [low_hit * jnp.where(high == float(t), 1.0, 0.0).astype(BF16) for t in range(tiles)]
            both = dot(jnp.concatenate(hits, axis=1), pair[...])
            seen = both[:, :samples] + both[:, samples:]
            back_ref[g * 16 + j] = (own[:, 0:1] * (1.0 + own[:, 1:2] * seen)).astype(BF16)
        return carry

    lax.fori_loop(0, groups, send, 0)
    temp_copy.wait()


def last_sweep(cols, cond, window, following, gain, turned):
    nodes, samples = gain.shape
    peers = turned.shape[0] * 16
    return pl.pallas_call(
        last_kernel,
        out_shape=(
            jax.ShapeDtypeStruct((nodes, samples), F32),
            jax.ShapeDtypeStruct((peers, CAP, samples), BF16),
        ),
        in_specs=[SMEM] + [VMEM] * 11,
        out_specs=(HBM, VMEM),
        scratch_shapes=[
            pltpu.VMEM((sum(part.shape[0] for part in window), samples), BF16),
            pltpu.VMEM((nodes, samples), F32),
            pltpu.VMEM((nodes, 2 * samples), BF16),
            pltpu.SemaphoreType.DMA,
        ],
        compiler_params=params(24),
        name="last_sweep",
    )(cols, cond, *window, *following, gain, turned)


def unpack_kernel(slot_ref, back_ref, out_hbm, wide, picked, out, sems):
    peers, _, samples = back_ref.shape
    for p in range(peers):
        wide[p * CAP : (p + 1) * CAP] = back_ref[p].astype(F32)
    chunks = slot_ref.shape[0] // PARTS

    def gather(r, carry):
        for lane in range(LANES):
            picked[pl.ds(r * LANES + lane, 1), :] = wide[pl.ds(slot_ref[r, lane], 1), :]
        return carry

    copies = []
    for g in range(PARTS):
        lax.fori_loop(g * chunks, (g + 1) * chunks, gather, 0)
        span = pl.ds(g * chunks * LANES, chunks * LANES)
        out[span, :] = picked[span, :].astype(BF16)
        copies.append(pltpu.make_async_copy(out.at[span], out_hbm.at[span], sems.at[g]))
        copies[g].start()
    for copy in copies:
        copy.wait()


def unpack(slots, back):
    peers, _, samples = back.shape
    count = slots.shape[0] * slots.shape[1]
    return pl.pallas_call(
        unpack_kernel,
        out_shape=jax.ShapeDtypeStruct((count, samples), BF16),
        in_specs=[SMEM, VMEM],
        out_specs=HBM,
        scratch_shapes=[
            pltpu.VMEM((peers * CAP, samples), F32),
            pltpu.VMEM((count, samples), F32),
            pltpu.VMEM((count, samples), BF16),
            pltpu.SemaphoreType.DMA((PARTS,)),
        ],
        compiler_params=params(24),
        name="unpack",
    )(slots, back)


def halo(head, tail):
    axes = ("dom", "blk")
    count = lax.axis_size(axes)
    left = lax.ppermute(tail, axes, [(i, (i + 1) % count) for i in range(count)])
    right = lax.ppermute(head, axes, [((i + 1) % count, i) for i in range(count)])
    return left, right


def body(current, resistivity, temp_coef, dest_part, dest_row, temp_old, heat_cap, conduction, block_cols):
    count, samples = current.shape
    peers = lax.axis_size("dom")
    blocks, size, _ = conduction.shape
    chunks = count // LANES
    width = HB * size
    left, right = halo(temp_old[:width].astype(BF16), temp_old[-width:].astype(BF16))
    send, slots = pack(
        dest_part.reshape(chunks, LANES),
        dest_row.reshape(chunks, LANES),
        resistivity.reshape(chunks, LANES),
        temp_coef.reshape(chunks, LANES),
        current,
        peers,
    )
    send, _, _ = lax.optimization_barrier((send, left, right))
    recv = lax.all_to_all(send, "dom", split_axis=0, concat_axis=0, tiled=True)
    devices = lax.axis_size(("dom", "blk"))
    first_block = lax.axis_index(("dom", "blk")) * blocks
    cols = jnp.mod(block_cols - first_block + HB, blocks * devices)
    base, gain, following, slope = first_sweep(cols, conduction, left, temp_old, right, heat_cap[:, None])
    nodes = temp_old.shape[0]
    outer = ((0, width), (nodes - width, width))
    inner = ((width, nodes - 2 * width),)
    next_head, next_tail, head, tail = gather_heat(recv, base, gain, following, slope, outer)
    left, right = halo(head, tail)
    next_mid, mid, turned = gather_heat(recv, base, gain, following, slope, inner, 1)
    window = (left, head, mid, tail, right)
    temp, back = last_sweep(cols, conduction, window, (next_head, next_mid, next_tail), gain, turned)
    returned = lax.all_to_all(back, "dom", split_axis=0, concat_axis=0, tiled=True)
    return temp, unpack(slots, returned)


def solution(mesh):
    both = ("dom", "blk")
    placed = (
        P(both, None),
        P(both),
        P(both),
        P(both, None),
        P(both),
        P(both, None),
        P(both),
        P(both, None, None),
        P(both, None),
    )
    return jax.shard_map(
        body,
        mesh=mesh,
        in_specs=placed,
        out_specs=(P(both, None), P(both, None)),
        check_vma=False,
    )
```

```python
import functools

import jax
import jax.numpy as jnp
from jax import lax
from jax.experimental import pallas as pl
from jax.experimental.pallas import tpu as pltpu
from jax.sharding import PartitionSpec as P

HB = 12
CAP = 128
META = 8
PARTS = 4
LANES = 128
F32 = jnp.float32
BF16 = jnp.bfloat16
VMEM = pl.BlockSpec(memory_space=pltpu.VMEM)
SMEM = pl.BlockSpec(memory_space=pltpu.SMEM)
HBM = pl.BlockSpec(memory_space=pltpu.HBM)


def params(mib):
    return pltpu.CompilerParams(vmem_limit_bytes=mib * 1024 * 1024)


def dot(a, b):
    return jnp.dot(a, b, preferred_element_type=F32)


def iota(shape, dim):
    return lax.broadcasted_iota(jnp.int32, shape, dim)


def pack_kernel(part_ref, row_ref, res_ref, coef_ref, cur_hbm, send_ref, slot_ref, slot_vmem, cur, wide, spread, ready, sem, out_sems):
    peers = send_ref.shape[0]
    fetch = pltpu.make_async_copy(cur_hbm, cur, sem.at[0])
    fetch.start()
    chunks = part_ref.shape[0]
    before = (iota((LANES, LANES), 0) < iota((LANES, LANES), 1)).astype(BF16)
    counter = jnp.concatenate([before, jnp.ones((LANES, LANES), BF16)], axis=1)
    carry = jnp.zeros((peers, LANES), F32)
    meta = jnp.zeros((4 * peers, LANES), F32)
    part = part_ref[...]
    row = row_ref[...]
    high = lax.shift_right_logical(row, 7).astype(F32)
    low = jnp.bitwise_and(row, 127).astype(F32)
    res = res_ref[...].astype(F32)
    coef = coef_ref[...].astype(F32)
    slots = []
    for r in range(chunks):
        hit = (iota((peers, LANES), 0) == part[r : r + 1]).astype(F32)
        counted = dot(hit.astype(BF16), counter)
        rank = jnp.sum(hit * (counted[:, :LANES] + carry), axis=0, keepdims=True)
        carry = carry + counted[:, LANES:]
        rank = rank.astype(jnp.int32)
        slots.append(part[r : r + 1] * CAP + rank)
        place = (iota((CAP, LANES), 0) == rank).astype(F32).astype(BF16)
        values = jnp.concatenate(
            [hit * res[r : r + 1], hit * coef[r : r + 1], hit * high[r : r + 1], hit * low[r : r + 1]], axis=0
        ).astype(BF16)
        meta = meta + lax.dot_general(values, place, (((1,), (1,)), ((), ())), preferred_element_type=F32)
    slot_vmem[...] = jnp.concatenate(slots, axis=0)
    copy = pltpu.make_async_copy(slot_vmem, slot_ref, sem.at[1])
    copy.start()
    spread[...] = jnp.zeros(spread.shape, F32)
    fetch.wait()
    wide[...] = cur[...].astype(F32)
    copy.wait()

    def scatter(r, carry):
        for lane in range(LANES):
            spread[pl.ds(slot_ref[r, lane], 1), :] = wide[pl.ds(r * LANES + lane, 1), :]
        return carry

    lax.fori_loop(0, chunks, scatter, 0)
    rows = [meta[i * peers : (i + 1) * peers] for i in range(4)]
    group = peers // PARTS
    copies = []
    for g in range(PARTS):
        for p in range(g * group, (g + 1) * group):
            own = jnp.concatenate([m[p : p + 1] for m in rows] + [jnp.zeros((META - 4, LANES), F32)], axis=0)
            ready[p, :CAP] = spread[p * CAP : (p + 1) * CAP].astype(BF16)
            ready[p, CAP:] = own.astype(BF16)
        span = pl.ds(g * group, group)
        copies.append(pltpu.make_async_copy(ready.at[span], send_ref.at[span], out_sems.at[g]))
        copies[g].start()
    for copy in copies:
        copy.wait()


def pack(part, row, res, coef, cur, peers):
    count, samples = cur.shape
    chunks = count // LANES
    return pl.pallas_call(
        pack_kernel,
        out_shape=(
            jax.ShapeDtypeStruct((peers, CAP + META, samples), BF16),
            jax.ShapeDtypeStruct((chunks, LANES), jnp.int32),
        ),
        in_specs=[VMEM] * 4 + [HBM],
        out_specs=(HBM, SMEM),
        scratch_shapes=[
            pltpu.VMEM((chunks, LANES), jnp.int32),
            pltpu.VMEM((count, samples), BF16),
            pltpu.VMEM((count, samples), F32),
            pltpu.VMEM((peers * CAP, samples), F32),
            pltpu.VMEM((peers, CAP + META, samples), BF16),
            pltpu.SemaphoreType.DMA((2,)),
            pltpu.SemaphoreType.DMA((PARTS,)),
        ],
        compiler_params=params(50),
        cost_estimate=pl.CostEstimate(flops=8_000_000_000, bytes_accessed=4_000_000, transcendentals=0),
        name="pack",
    )(part, row, res, coef, cur)


def apply_blocks(cols_ref, cond_ref, window_ref, r):
    size = cond_ref.shape[1]
    picked = []
    for k in range(cols_ref.shape[1]):
        start = pl.multiple_of(cols_ref[r, k] * size, size)
        picked.append(window_ref[pl.ds(start, size), :])
    return dot(cond_ref[r], jnp.concatenate(picked, axis=0))


def fill(window_ref, *parts):
    start = 0
    for ref in parts:
        window_ref[start : start + ref.shape[0]] = ref[...].astype(BF16)
        start += ref.shape[0]


def first_kernel(cols_ref, cond_ref, left_ref, old_ref, right_ref, cap_ref, base_ref, gain_ref, next_ref, slope_ref, window_ref):
    fill(window_ref, left_ref, old_ref, right_ref)
    blocks, size, _ = cond_ref.shape
    samples = window_ref.shape[1]
    eye = iota((size, size), 0) == iota((size, size), 1)

    def step(r, carry):
        rows = pl.ds(pl.multiple_of(r * size, size), size)
        applied = apply_blocks(cols_ref, cond_ref, window_ref, r)
        corner = cond_ref[r, :, :size].astype(F32)
        diag = jnp.sum(jnp.where(eye, corner, 0.0), axis=1, keepdims=True)
        cap = cap_ref[rows, :]
        gain = jnp.broadcast_to(1.0 / (diag + cap), (size, samples))
        cap = jnp.broadcast_to(cap, (size, samples))
        old = old_ref[rows, :]
        base = old - applied * gain
        share = cap * gain
        base_ref[rows, :] = base
        gain_ref[rows, :] = gain
        next_ref[rows, :] = base * (1.0 - share) + share * old
        slope_ref[rows, :] = gain * (2.0 - share)
        return carry

    lax.fori_loop(0, blocks, step, 0, unroll=8)


def first_sweep(cols, cond, left, old, right, cap):
    nodes, samples = old.shape
    return pl.pallas_call(
        first_kernel,
        out_shape=(jax.ShapeDtypeStruct((nodes, samples), F32),) * 4,
        in_specs=[SMEM] + [VMEM] * 5,
        out_specs=(VMEM,) * 4,
        scratch_shapes=[pltpu.VMEM((nodes + 2 * left.shape[0], samples), BF16)],
        compiler_params=params(48),
        cost_estimate=pl.CostEstimate(flops=8_000_000_000, bytes_accessed=8_000_000, transcendentals=0),
        name="first_sweep",
    )(cols, cond, left, old, right, cap)


STEP = 8


def gather_kernel(spans, turning, recv_hbm, base_hbm, gain_hbm, next_hbm, slope_hbm, *rest):
    count = len(spans)
    next_refs, low_refs = rest[:count], rest[count : 2 * count]
    turned_refs = rest[2 * count : 2 * count + turning]
    recv_ref, node_in, chosen, high, values, recv_sems, sems = rest[2 * count + turning :]
    peers = recv_ref.shape[0]
    group = peers // PARTS
    samples = node_in.shape[2]
    arrivals = []
    for g in range(PARTS):
        span = pl.ds(g * group, group)
        arrivals.append(pltpu.make_async_copy(recv_hbm.at[span], recv_ref.at[span], recv_sems.at[g]))
        arrivals[g].start()
    copies, offsets, offset = [], [], 0
    for k, (first, size) in enumerate(spans):
        for i, ref in enumerate((base_hbm, gain_hbm, next_hbm, slope_hbm)):
            target = node_in.at[i, pl.ds(offset, size)]
            copies.append(pltpu.make_async_copy(ref.at[pl.ds(first, size)], target, sems.at[4 * k + i]))
        offsets.append(offset)
        offset += size
    for copy in copies:
        copy.start()
    sub = iota((LANES, LANES), 0).astype(F32)

    def split(p, carry):
        rows = pl.ds(pl.multiple_of(p * CAP, CAP), CAP)
        cur = recv_ref[p, :CAP].astype(F32)
        square = cur * cur
        top = square.astype(BF16)
        rest = (square - top.astype(F32)).astype(BF16)
        values[rows, :] = jnp.concatenate([top, rest], axis=1)
        meta = recv_ref[p, CAP:].astype(F32)
        chosen[:, rows] = jnp.where(sub == meta[3:4], meta[0:1], 0.0).astype(BF16)
        high[:, rows] = jnp.broadcast_to(meta[2:3], (16, CAP)).astype(BF16)
        return carry

    for g in range(PARTS):
        arrivals[g].wait()
        lax.fori_loop(g * group, (g + 1) * group, split, 0, unroll=4)
    for ref in turned_refs:
        for g in range(peers // 16):
            stacked = jnp.concatenate([recv_ref[g * 16 + j, CAP:].astype(F32) for j in range(16)], axis=0)
            ref[g] = stacked.T
    part = peers * CAP // STEP
    for copy in copies:
        copy.wait()
    for k, (first, size) in enumerate(spans):
        mt = next(m for m in (6, 4, 3, 2, 1) if size // LANES % m == 0)

        def tile(t, carry):
            both = jnp.zeros((mt * LANES, 2 * samples), F32)
            for c in range(STEP):
                cols = slice(c * part, (c + 1) * part)
                own_base = chosen[:, cols]
                own_high = high[:, cols]
                hits = []
                for i in range(mt):
                    own = (first // LANES + t * mt + i).astype(F32).astype(BF16)
                    hit = (own_high == own).astype(BF16)
                    hits.append(own_base * jnp.concatenate([hit] * (LANES // 16), axis=0))
                both = both + dot(jnp.concatenate(hits, axis=0), values[cols, :])
            start = pl.multiple_of(t * mt * LANES, LANES)
            rows = pl.ds(start, mt * LANES)
            here = pl.ds(offsets[k] + start, mt * LANES)
            heat = both[:, :samples] + both[:, samples:]
            field = node_in[0, here, :] + heat * node_in[1, here, :]
            next_refs[k][rows, :] = node_in[2, here, :] + heat * node_in[3, here, :]
            low_refs[k][rows, :] = field.astype(BF16)
            return carry

        lax.fori_loop(0, size // LANES // mt, tile, 0)


def gather_heat(recv, base, gain, following, slope, spans, turning=0):
    samples = base.shape[1]
    slots = recv.shape[0] * CAP
    count = sum(size for _, size in spans)
    shapes = [jax.ShapeDtypeStruct((size, samples), kind) for kind in (F32, BF16) for _, size in spans]
    shapes += [jax.ShapeDtypeStruct((recv.shape[0] // 16, CAP, LANES), F32)] * turning
    return pl.pallas_call(
        functools.partial(gather_kernel, spans, turning),
        out_shape=tuple(shapes),
        in_specs=[HBM] * 5,
        out_specs=(VMEM,) * len(shapes),
        scratch_shapes=[
            pltpu.VMEM(recv.shape, BF16),
            pltpu.VMEM((4, count, samples), F32),
            pltpu.VMEM((LANES, slots), BF16),
            pltpu.VMEM((16, slots), BF16),
            pltpu.VMEM((slots, 2 * samples), BF16),
            pltpu.SemaphoreType.DMA((PARTS,)),
            pltpu.SemaphoreType.DMA((4 * len(spans),)),
        ],
        compiler_params=params(52),
        cost_estimate=pl.CostEstimate(flops=4 * slots * count * samples, bytes_accessed=8_000_000, transcendentals=0),
        name="gather_heat",
    )(recv, base, gain, following, slope)


def last_kernel(cols_ref, cond_ref, left_ref, head_ref, mid_ref, tail_ref, right_ref, next_head, next_mid, next_tail, gain_ref, turned_ref, temp_hbm, back_ref, window_ref, temp, pair, temp_sem):
    fill(window_ref, left_ref, head_ref, mid_ref, tail_ref, right_ref)
    blocks, size, _ = cond_ref.shape
    nodes, samples = gain_ref.shape
    groups = turned_ref.shape[0]
    tiles = nodes // LANES

    first = 0
    for ref in (next_head, next_mid, next_tail):

        def step(i, carry):
            r = first + i
            rows = pl.ds(pl.multiple_of(r * size, size), size)
            applied = apply_blocks(cols_ref, cond_ref, window_ref, r)
            field = ref[pl.ds(pl.multiple_of(i * size, size), size), :] - applied * gain_ref[rows, :]
            temp[rows, :] = field
            top = field.astype(BF16)
            rest = (field - top.astype(F32)).astype(BF16)
            pair[rows, :] = jnp.concatenate([top, rest], axis=1)
            return carry

        lax.fori_loop(0, ref.shape[0] // size, step, 0, unroll=8 if ref is next_mid else 12)
        first += ref.shape[0] // size
    temp_copy = pltpu.make_async_copy(temp, temp_hbm, temp_sem)
    temp_copy.start()
    lane = iota((CAP, LANES), 1).astype(F32)

    def send(g, carry):
        for j in range(16):
            own = turned_ref[g, :, j * META : j * META + 4]
            low = jnp.broadcast_to(own[:, 3:4], (CAP, LANES))
            low_hit = jnp.where(low == lane, 1.0, 0.0).astype(BF16)
            high = jnp.broadcast_to(own[:, 2:3], (CAP, LANES))
            hits = [low_hit * jnp.where(high == float(t), 1.0, 0.0).astype(BF16) for t in range(tiles)]
            both = dot(jnp.concatenate(hits, axis=1), pair[...])
            seen = both[:, :samples] + both[:, samples:]
            back_ref[g * 16 + j] = (own[:, 0:1] * (1.0 + own[:, 1:2] * seen)).astype(BF16)
        return carry

    lax.fori_loop(0, groups, send, 0)
    temp_copy.wait()


def last_sweep(cols, cond, window, following, gain, turned):
    nodes, samples = gain.shape
    peers = turned.shape[0] * 16
    return pl.pallas_call(
        last_kernel,
        out_shape=(
            jax.ShapeDtypeStruct((nodes, samples), F32),
            jax.ShapeDtypeStruct((peers, CAP, samples), BF16),
        ),
        in_specs=[SMEM] + [VMEM] * 11,
        out_specs=(HBM, VMEM),
        scratch_shapes=[
            pltpu.VMEM((sum(part.shape[0] for part in window), samples), BF16),
            pltpu.VMEM((nodes, samples), F32),
            pltpu.VMEM((nodes, 2 * samples), BF16),
            pltpu.SemaphoreType.DMA,
        ],
        compiler_params=params(24),
        name="last_sweep",
    )(cols, cond, *window, *following, gain, turned)


def unpack_kernel(slot_ref, back_ref, out_hbm, wide, picked, out, sems):
    peers, _, samples = back_ref.shape
    for p in range(peers):
        wide[p * CAP : (p + 1) * CAP] = back_ref[p].astype(F32)
    chunks = slot_ref.shape[0] // PARTS

    def gather(r, carry):
        for lane in range(LANES):
            picked[pl.ds(r * LANES + lane, 1), :] = wide[pl.ds(slot_ref[r, lane], 1), :]
        return carry

    copies = []
    for g in range(PARTS):
        lax.fori_loop(g * chunks, (g + 1) * chunks, gather, 0)
        span = pl.ds(g * chunks * LANES, chunks * LANES)
        out[span, :] = picked[span, :].astype(BF16)
        copies.append(pltpu.make_async_copy(out.at[span], out_hbm.at[span], sems.at[g]))
        copies[g].start()
    for copy in copies:
        copy.wait()


def unpack(slots, back):
    peers, _, samples = back.shape
    count = slots.shape[0] * slots.shape[1]
    return pl.pallas_call(
        unpack_kernel,
        out_shape=jax.ShapeDtypeStruct((count, samples), BF16),
        in_specs=[SMEM, VMEM],
        out_specs=HBM,
        scratch_shapes=[
            pltpu.VMEM((peers * CAP, samples), F32),
            pltpu.VMEM((count, samples), F32),
            pltpu.VMEM((count, samples), BF16),
            pltpu.SemaphoreType.DMA((PARTS,)),
        ],
        compiler_params=params(24),
        name="unpack",
    )(slots, back)


def halo(head, tail):
    axes = ("dom", "blk")
    count = lax.axis_size(axes)
    left = lax.ppermute(tail, axes, [(i, (i + 1) % count) for i in range(count)])
    right = lax.ppermute(head, axes, [((i + 1) % count, i) for i in range(count)])
    return left, right


def body(current, resistivity, temp_coef, dest_part, dest_row, temp_old, heat_cap, conduction, block_cols):
    count, samples = current.shape
    peers = lax.axis_size("dom")
    blocks, size, _ = conduction.shape
    chunks = count // LANES
    width = HB * size
    left, right = halo(temp_old[:width].astype(BF16), temp_old[-width:].astype(BF16))
    send, slots = pack(
        dest_part.reshape(chunks, LANES),
        dest_row.reshape(chunks, LANES),
        resistivity.reshape(chunks, LANES),
        temp_coef.reshape(chunks, LANES),
        current,
        peers,
    )
    send, _, _ = lax.optimization_barrier((send, left, right))
    recv = lax.all_to_all(send, "dom", split_axis=0, concat_axis=0, tiled=True)
    devices = lax.axis_size(("dom", "blk"))
    first_block = lax.axis_index(("dom", "blk")) * blocks
    cols = jnp.mod(block_cols - first_block + HB, blocks * devices)
    base, gain, following, slope = first_sweep(cols, conduction, left, temp_old, right, heat_cap[:, None])
    nodes = temp_old.shape[0]
    outer = ((0, width), (nodes - width, width))
    inner = ((width, nodes - 2 * width),)
    next_head, next_tail, head, tail = gather_heat(recv, base, gain, following, slope, outer)
    left, right = halo(head, tail)
    next_mid, mid, turned = gather_heat(recv, base, gain, following, slope, inner, 1)
    window = (left, head, mid, tail, right)
    temp, back = last_sweep(cols, conduction, window, (next_head, next_mid, next_tail), gain, turned)
    returned = lax.all_to_all(back, "dom", split_axis=0, concat_axis=0, tiled=True)
    return temp, unpack(slots, returned)


def solution(mesh):
    both = ("dom", "blk")
    placed = (
        P(both, None),
        P(both),
        P(both),
        P(both, None),
        P(both),
        P(both, None),
        P(both),
        P(both, None, None),
        P(both, None),
    )
    return jax.shard_map(
        body,
        mesh=mesh,
        in_specs=placed,
        out_specs=(P(both, None), P(both, None)),
        check_vma=False,
    )
```
